512 devices in a mesh: dp: 16 (over y, core), slab: 16 (over z, x_lo), chan: 2 (over x_hi).
Axes of the slice: x: 4 (x_hi: 2, x_lo: 2; x = x_hi * 2 + x_lo), y: 8, z: 8, core: 2. Of those that a mesh axis runs over, the one named last changes fastest.
Arguments:
- center_in: bfloat16 [16, 64, 128, 256], P('dp', 'slab', None, 'chan'), may hold values from 0 to 2
- radius_in: bfloat16 [16, 64, 128, 256], P('dp', 'slab', None, 'chan'), may hold values from 0.049804688 to 1
- hidden_center: bfloat16 [16, 64, 128, 256], P('dp', 'slab', None, 'chan'), may hold values from 0 to 2
- hidden_radius: bfloat16 [16, 64, 128, 256], P('dp', 'slab', None, 'chan'), may hold values from 0 to 1
- state_one: int32 [16, 64, 128, 256], P('dp', 'slab', None, 'chan'), may hold values from 0 to 2
- state_two: int32 [16, 64, 128, 256], P('dp', 'slab', None, 'chan'), may hold values from 0 to 2
- weight_one: bfloat16 [3, 3, 256, 256], P(None, None, None, 'chan'), may hold values from -0.125 to 0.125
- weight_two: bfloat16 [3, 3, 256, 256], P(None, None, None, 'chan'), may hold values from -0.125 to 0.125
- grad_center: bfloat16 [16, 64, 128, 256], P('dp', 'slab', None, 'chan'), may hold values from -6 to 6
- grad_radius: bfloat16 [16, 64, 128, 256], P('dp', 'slab', None, 'chan'), may hold values from -6 to 6
Outputs:
- input_grad_center: float32 [16, 64, 128, 256], P('dp', 'slab', None, 'chan')
- input_grad_radius: float32 [16, 64, 128, 256], P('dp', 'slab', None, 'chan')
- kernel_grad_one: bfloat16 [3, 3, 256, 256], P(None, None, None, 'chan')
- kernel_grad_two: bfloat16 [3, 3, 256, 256], P(None, None, None, 'chan')
The draws below stay inside these ranges and needn't reach their ends.
Inputs may be any that keep to these rules, and one draw needn't show every extreme that they name: `state_one`: 0 marks an inactive unit, 1 an active one, 2 an unstable one. `state_two`: 0 marks an inactive unit, 1 an active one, 2 an unstable one.
All inputs are finite; a program needn't handle non-finite values.
Results may differ from the reference program's by a relative error of at most 0.0054.
Values may be sent and summed in bfloat16 or wider, within the bound.
A program may use at most 64 MiB of HBM per device.

```python
import math
import jax
import jax.numpy as jnp
from jax import lax

C = 256
WIDTH = 128
IMAGES = 16
H = 64


def set_ends(drawn, own_key, smallest, largest):
    longest = drawn.shape.index(max(drawn.shape))
    spots = []
    for shift in (0, 1):
        where = [jax.random.randint(jax.random.fold_in(own_key, axis), (), 0, length) for axis, length in enumerate(drawn.shape)]
        where[longest] = (where[longest] + shift) % drawn.shape[longest]
        spots.append(tuple(where))
    return drawn.at[spots[0]].set(smallest).at[spots[1]].set(largest)


def block_levels(key, shape, split, low, high):
    loudness = 1.0
    for position, parts in split:
        steps = jax.random.uniform(jax.random.fold_in(jax.random.fold_in(key, 6), position), (parts,), jnp.float32, low / len(split), high / len(split))
        loudness = loudness * jnp.repeat(jnp.exp(steps), shape[position] // parts).reshape((-1,) + (1,) * (len(shape) - 1 - position))
    return loudness


def scatter_about(rng, dims, scale, reach, shards=(), dtype=jnp.bfloat16):
    gain = block_levels(rng, dims, shards, -0.22, 0.18) if shards else 1.0
    drawn = jax.random.normal(rng, dims, jnp.float32) * scale * gain
    return jnp.minimum(jnp.maximum(drawn, -reach), reach).astype(dtype)


def setup_inputs(seed: int = 0) -> dict:
    key_list = jax.random.split(jax.random.key(seed), 11)
    center_in = jnp.clip(2.0 * jax.random.uniform(key_list[0], (IMAGES, H, WIDTH, C), jnp.float32) ** block_levels(key_list[0], (IMAGES, H, WIDTH, C), ((0, 16), (1, 16), (3, 2)), -0.2, 0.2), 0.0, 2.0).astype(jnp.bfloat16)
    radius_in = jnp.clip(0.049804688 + 0.9501953 * jax.random.uniform(key_list[1], (IMAGES, H, WIDTH, C), jnp.float32) ** block_levels(key_list[1], (IMAGES, H, WIDTH, C), ((0, 16), (1, 16), (3, 2)), -0.2, 0.2), 0.049804688, 1.0).astype(jnp.bfloat16)
    hidden_center = jnp.clip(2.0 * jax.random.uniform(key_list[2], (IMAGES, H, WIDTH, C), jnp.float32) ** block_levels(key_list[2], (IMAGES, H, WIDTH, C), ((0, 16), (1, 16), (3, 2)), -0.2, 0.2), 0.0, 2.0).astype(jnp.bfloat16)
    hidden_radius = jnp.clip(1.0 * jax.random.uniform(key_list[3], (IMAGES, H, WIDTH, C), jnp.float32) ** block_levels(key_list[3], (IMAGES, H, WIDTH, C), ((0, 16), (1, 16), (3, 2)), -0.2, 0.2), 0.0, 1.0).astype(jnp.bfloat16)
    state_one = set_ends(jax.random.randint(key_list[4], (IMAGES, H, WIDTH, C), 0, 3), jax.random.fold_in(key_list[4], 1), 0, 2).astype(jnp.int32)
    state_two = set_ends(jax.random.randint(key_list[5], (IMAGES, H, WIDTH, C), 0, 3), jax.random.fold_in(key_list[5], 1), 0, 2).astype(jnp.int32)
    weight_one = scatter_about(key_list[6], (3, 3, C, C), (9 * C) ** -0.5, 0.125, ((3, 2),))
    weight_two = scatter_about(key_list[7], (3, 3, C, C), (9 * C) ** -0.5, 0.125, ((3, 2),))
    grad_center = scatter_about(key_list[8], (IMAGES, H, WIDTH, C), 1.0, 6.0, ((0, 16), (1, 16), (3, 2)))
    grad_radius = scatter_about(key_list[9], (IMAGES, H, WIDTH, C), 1.0, 6.0, ((0, 16), (1, 16), (3, 2)))
    return {"center_in": center_in, "radius_in": radius_in, "hidden_center": hidden_center, "hidden_radius": hidden_radius, "state_one": state_one, "state_two": state_two, "weight_one": weight_one, "weight_two": weight_two, "grad_center": grad_center, "grad_radius": grad_radius}


def relu_back(grad_c, grad_r, states):
    average = 0.5 * (grad_c + grad_r)
    keep_c = jnp.where(states == 1, grad_c, jnp.where(states == 2, average, 0.0))
    keep_r = jnp.where(states == 1, grad_r, jnp.where(states == 2, average, 0.0))
    return (keep_c.astype(jnp.bfloat16), keep_r.astype(jnp.bfloat16))

def layer_back(grad_c, grad_r, act_c, act_r, weight):
    row_count, col_count = (grad_c.shape[0], grad_c.shape[1])
    padded_c = jnp.pad(grad_c.astype(jnp.float32), ((1, 1), (1, 1), (0, 0)))
    padded_r = jnp.pad(grad_r.astype(jnp.float32), ((1, 1), (1, 1), (0, 0)))
    weight_f = weight.astype(jnp.float32)
    magnitude = jnp.abs(weight_f)
    weight_sign = jnp.sign(weight_f)
    act_cf = act_c.astype(jnp.float32)
    act_rf = act_r.astype(jnp.float32)
    back_c = jnp.zeros((row_count, col_count, weight.shape[2]), jnp.float32)
    back_r = jnp.zeros((row_count, col_count, weight.shape[2]), jnp.float32)
    taps_c = []
    taps_r = []
    for row_tap in range(3):
        for col_tap in range(3):
            window_c = padded_c[2 - row_tap:2 - row_tap + row_count, 2 - col_tap:2 - col_tap + col_count]
            window_r = padded_r[2 - row_tap:2 - row_tap + row_count, 2 - col_tap:2 - col_tap + col_count]
            back_c = back_c + jnp.einsum('hwo,io->hwi', window_c, weight_f[row_tap, col_tap])
            back_r = back_r + jnp.einsum('hwo,io->hwi', window_r, magnitude[row_tap, col_tap])
            taps_c.append(jnp.einsum('hwi,hwo->io', act_cf, window_c))
            taps_r.append(jnp.einsum('hwi,hwo->io', act_rf, window_r))
    center_taps = jnp.stack(taps_c).reshape(weight.shape)
    radius_taps = jnp.stack(taps_r).reshape(weight.shape)
    return (back_c, back_r, center_taps + weight_sign * radius_taps)

def reference(center_in, radius_in, hidden_center, hidden_radius, state_one, state_two, weight_one, weight_two, grad_center, grad_radius):

    def one_image(items):
        c_in, r_in, h_c, h_r, s_one, s_two, g_c, g_r = items
        skip_c, skip_r = relu_back(g_c.astype(jnp.float32), g_r.astype(jnp.float32), s_two)
        back_c, back_r, grad_two = layer_back(skip_c, skip_r, h_c, h_r, weight_two)
        inner_c, inner_r = relu_back(back_c, back_r, s_one)
        back_c, back_r, grad_one = layer_back(inner_c, inner_r, c_in, r_in, weight_one)
        return (skip_c.astype(jnp.float32) + back_c, skip_r.astype(jnp.float32) + back_r, grad_one, grad_two)
    out_c, out_r, grads_one, grads_two = lax.map(one_image, (center_in, radius_in, hidden_center, hidden_radius, state_one, state_two, grad_center, grad_radius))
    loss_scale = 1.0 / math.sqrt(IMAGES * H * WIDTH)
    kernel_one = (loss_scale * lax.optimization_barrier(jnp.sum(grads_one, axis=0))).astype(jnp.bfloat16)
    kernel_two = (loss_scale * lax.optimization_barrier(jnp.sum(grads_two, axis=0))).astype(jnp.bfloat16)
    return (out_c, out_r, kernel_one, kernel_two)
```

```python
import functools
import math

import jax
import jax.numpy as jnp
from jax import lax
from jax.experimental import pallas as pl
from jax.experimental.pallas import tpu as pltpu
from jax.sharding import PartitionSpec as P

MESH = pl.DeviceIdType.MESH
F32 = jnp.float32
BF16 = jnp.bfloat16


def relu_back(grad_c, grad_r, states):
    average = 0.5 * (grad_c + grad_r)
    keep_c = jnp.where(states == 1, grad_c, jnp.where(states == 2, average, 0.0))
    keep_r = jnp.where(states == 1, grad_r, jnp.where(states == 2, average, 0.0))
    return keep_c.astype(BF16), keep_r.astype(BF16)


def kernel(
    sizes,
    center_in,
    radius_in,
    hidden_center,
    hidden_radius,
    state_one,
    state_two,
    weight_one,
    weight_two,
    grad_center,
    grad_radius,
    out_c,
    out_r,
    out_k,
    grads,
    states,
    wcat,
    wabs,
    act,
    act_t,
    skip,
    inner,
    halo,
    cols,
    part_own,
    part_send,
    part_recv,
    final,
    k_full,
    k_send,
    k_recv,
    k_mine,
    got_one,
    two,
    got_two,
    result,
    in_sem,
    w_sem,
    act_sem,
    halo_ss,
    halo_rs,
    act_ss,
    act_rs,
    part_ss,
    part_rs,
    core_sem,
    one_ss,
    one_rs,
    two_ss,
    two_rs,
    back_ss,
    back_rs,
    fwd_ss,
    fwd_rs,
    out_sem,
    k_out_sem,
):
    ny, nz, rows, width, scale = sizes
    pix = rows * width
    dp, slab, chan = lax.axis_index("dp"), lax.axis_index("slab"), lax.axis_index("chan")
    y, core = lax.div(dp, 2), lax.rem(dp, 2)
    z, x_lo = lax.div(slab, 2), lax.rem(slab, 2)
    slabs = 2 * nz
    first = core == 0
    members = 2 * ny
    chunk = 256 // members
    pos_one = jnp.where(first, y, z) * 2 + x_lo
    pos_two = jnp.where(first, z, y)

    def one_dev(j):
        a = lax.div(j, 2)
        return (
            jnp.where(first, a, y) * 2 + core,
            jnp.where(first, z, a) * 2 + lax.rem(j, 2),
            chan,
        )

    def two_dev(j):
        return (jnp.where(first, y, j) * 2 + core, jnp.where(first, j, z) * 2 + x_lo, chan)

    partner = (dp, slab, 1 - chan)
    sibling = (y * 2 + 1 - core, slab, chan)
    above = (dp, lax.rem(slab + slabs - 1, slabs), chan)
    below = (dp, lax.rem(slab + 1, slabs), chan)

    def load(src, dst, sem):
        copy = pltpu.make_async_copy(src, dst, sem)
        copy.start()
        return copy

    c_grad = load(grad_center, grads.at[0], in_sem.at[0])
    r_grad = load(grad_radius, grads.at[1], in_sem.at[1])
    s_two = load(state_two, states.at[1], in_sem.at[2])

    barrier = pltpu.get_barrier_semaphore()
    for peer in (partner, sibling, above, below):
        pl.semaphore_signal(barrier, inc=1, device_id=peer, device_id_type=MESH)

    @pl.loop(1, members)
    def _(d):
        pl.semaphore_signal(
            barrier, inc=1, device_id=one_dev(lax.rem(pos_one + d, members)), device_id_type=MESH
        )

    @pl.loop(1, nz)
    def _(d):
        pl.semaphore_signal(
            barrier, inc=1, device_id=two_dev(lax.rem(pos_two + d, nz)), device_id_type=MESH
        )

    w_rows = (
        pl.ds(pl.multiple_of(chan * 128, 128), 128),
        pl.ds(pl.multiple_of((1 - chan) * 128, 128), 128),
    )

    def load_w(src, layer):
        for tap in range(9):
            for half in range(2):
                pltpu.make_async_copy(
                    src.at[tap, w_rows[half], :],
                    wcat.at[layer, pl.ds(128 * half, 128), pl.ds(128 * tap, 128)],
                    w_sem.at[layer],
                ).start()

    def wait_w(layer):
        pltpu.make_async_copy(wcat.at[layer], wcat.at[layer], w_sem.at[layer]).wait()

    load_w(weight_two, 1)
    acts = ((center_in, radius_in), (hidden_center, hidden_radius))
    act_own = [[load(acts[l][x], act.at[l, x, 0], act_sem.at[2 * l + x]) for x in range(2)] for l in range(2)]
    s_one = load(state_one, states.at[0], in_sem.at[3])
    load_w(weight_one, 0)

    c_grad.wait()
    r_grad.wait()
    s_two.wait()
    for r in range(rows):
        at = pl.ds(r * width, width)
        sc, sr = relu_back(grads[0, at, :].astype(F32), grads[1, at, :].astype(F32), states[1, at, :])
        skip[0, at, :] = sc
        skip[1, at, :] = sr

    column = lax.broadcasted_iota(jnp.int32, (width, 128), 0)

    def place(x, row, value):
        wide = value.astype(F32)
        later = jnp.where(column == width - 1, 0.0, pltpu.roll(wide, width - 1, 0)).astype(BF16)
        sooner = jnp.where(column == 0, 0.0, pltpu.roll(wide, 1, 0)).astype(BF16)
        for a in range(3):
            r = row - 2 + a
            if 0 <= r < rows:
                for b, shifted in enumerate((later, value, sooner)):
                    cols[x, pl.ds(r * width, width), pl.ds(128 * (3 * a + b), 128)] = shifted

    def place_inside(source):
        for x in range(2):
            for r in range(rows):
                place(x, r + 1, source[x, pl.ds(r * width, width), :])

    def send_halo(source, layer):
        up = pltpu.make_async_remote_copy(
            source.at[:, pl.ds(0, width), :], halo.at[layer, 1],
            halo_ss.at[layer, 0], halo_rs.at[layer, 1], device_id=above, device_id_type=MESH,
        )
        down = pltpu.make_async_remote_copy(
            source.at[:, pl.ds((rows - 1) * width, width), :], halo.at[layer, 0],
            halo_ss.at[layer, 1], halo_rs.at[layer, 0], device_id=below, device_id_type=MESH,
        )
        up.start()
        down.start()
        return up, down

    def place_halo(copies, layer):
        copies[0].wait()
        copies[1].wait()
        top = slab > 0
        bottom = slab < slabs - 1
        for x in range(2):
            above_row = halo[layer, 0, x].astype(F32)
            below_row = halo[layer, 1, x].astype(F32)
            place(x, 0, jnp.where(top, above_row, 0.0).astype(BF16))
            place(x, rows + 1, jnp.where(bottom, below_row, 0.0).astype(BF16))

    def send_act(layer):
        copies = []
        for x in range(2):
            copy = pltpu.make_async_remote_copy(
                act.at[layer, x, 0], act.at[layer, x, 1],
                act_ss.at[layer, x], act_rs.at[layer, x], device_id=partner, device_id_type=MESH,
            )
            act_own[layer][x].wait()
            copy.start()
            copies.append(copy)
        return copies

    def convolve(layer):
        copies = []
        for x in range(2):
            weight = wcat[layer] if x == 0 else wabs[layer]
            both = lax.dot_general(
                cols[x], weight, (((1,), (1,)), ((), ())), preferred_element_type=F32
            )
            part_own[x] = both[:, :128]
            part_send[layer, x] = both[:, 128:].astype(BF16)
            copy = pltpu.make_async_remote_copy(
                part_send.at[layer, x], part_recv.at[layer, x],
                part_ss.at[layer, x], part_rs.at[layer, x], device_id=partner, device_id_type=MESH,
            )
            copy.start()
            copies.append(copy)
        return copies

    def turn_own(layer):
        for x in range(2):
            act_t[x, :128, :] = act[layer, x, 0].T

    def kernel_terms(layer, copies):
        for x in range(2):
            copies[x].wait()
            act_t[x, 128:, :] = act[layer, x, 1].T
        for a in range(3):
            at = pl.ds(384 * a, 384)
            kc = jnp.dot(act_t[0], cols[0, :, at], preferred_element_type=F32)
            kr = jnp.dot(act_t[1], cols[1, :, at], preferred_element_type=F32)
            w = wcat[layer, :, at].astype(F32)
            kr = jnp.where(w > 0.0, kr, jnp.where(w < 0.0, -kr, 0.0))
            k_full[1 - layer, :, at] = scale * (kc + kr)

    place_inside(skip)
    pl.semaphore_wait(barrier, 4 + members - 1 + nz - 1)
    halo_two = send_halo(skip, 1)
    act_two = send_act(1)
    wait_w(1)
    wabs[1] = jnp.abs(wcat[1])
    turn_own(1)
    place_halo(halo_two, 1)
    part_two = convolve(1)
    act_one = send_act(0)
    kernel_terms(1, act_two)

    turn_own(0)
    wait_w(0)
    wabs[0] = jnp.abs(wcat[0])
    s_one.wait()
    for copy in part_two:
        copy.wait()
    for r in range(rows):
        at = pl.ds(r * width, width)
        back_c = part_own[0, at, :] + part_recv[1, 0, at, :].astype(F32)
        back_r = part_own[1, at, :] + part_recv[1, 1, at, :].astype(F32)
        ic, ir = relu_back(back_c, back_r, states[0, at, :])
        inner[0, at, :] = ic
        inner[1, at, :] = ir
    halo_one = send_halo(inner, 0)
    place_inside(inner)
    place_halo(halo_one, 0)
    kernel_terms(0, act_one)

    k_send[...] = k_full[1 - core].astype(BF16)
    to_core = pltpu.make_async_remote_copy(
        k_send, k_recv, core_sem.at[0], core_sem.at[1], device_id=sibling, device_id_type=MESH
    )
    to_core.start()
    part_one = convolve(0)
    to_core.wait()
    k_mine[...] = (k_full[core] + k_recv[...].astype(F32)).astype(BF16)

    def rows_of(j):
        return pl.ds(pl.multiple_of(j * chunk, chunk), chunk)

    def one_copy(d):
        j = lax.rem(pos_one + d, members)
        return pltpu.make_async_remote_copy(
            k_mine.at[rows_of(j), :], got_one.at[pos_one],
            one_ss.at[d - 1], one_rs.at[d - 1], device_id=one_dev(j), device_id_type=MESH,
        )

    @pl.loop(1, members)
    def _(d):
        one_copy(d).start()

    got_one[pos_one] = k_mine[rows_of(pos_one), :]

    outs = []
    for x, out in enumerate((out_c, out_r)):
        part_one[x].wait()
        final[x] = (
            skip[x].astype(F32) + part_own[x] + part_recv[0, x].astype(F32)
        )
        outs.append(load(final.at[x], out, out_sem.at[x]))

    @pl.loop(1, members)
    def _(d):
        one_copy(d).wait()

    total = got_one[0].astype(F32)
    for j in range(1, members):
        total = total + got_one[j].astype(F32)
    two[...] = total.astype(BF16)

    def two_copy(d):
        return pltpu.make_async_remote_copy(
            two, got_two.at[pos_two], two_ss.at[d - 1], two_rs.at[d - 1],
            device_id=two_dev(lax.rem(pos_two + d, nz)), device_id_type=MESH,
        )

    @pl.loop(1, nz)
    def _(d):
        two_copy(d).start()

    got_two[pos_two] = two[...]

    @pl.loop(1, nz)
    def _(d):
        two_copy(d).wait()

    total = got_two[0].astype(F32)
    for j in range(1, nz):
        total = total + got_two[j].astype(F32)
    result[core, rows_of(pos_one), :] = total.astype(BF16)

    def back_copy(d):
        j = lax.rem(pos_one + d, members)
        mine = result.at[core, rows_of(pos_one), :]
        return pltpu.make_async_remote_copy(
            mine, mine, back_ss.at[d - 1], back_rs.at[d - 1], device_id=one_dev(j), device_id_type=MESH
        )

    def fwd_copy(d):
        there = result.at[core, rows_of(lax.rem(pos_one - d + members, members)), :]
        return pltpu.make_async_remote_copy(
            there, there, fwd_ss.at[d], fwd_rs.at[d], device_id=sibling, device_id_type=MESH
        )

    def back_wait(d):
        there = result.at[core, rows_of(lax.rem(pos_one - d + members, members)), :]
        return pltpu.make_async_remote_copy(
            there, there, back_ss.at[d - 1], back_rs.at[d - 1], device_id=sibling, device_id_type=MESH
        )

    @pl.loop(1, members)
    def _(d):
        back_copy(d).start()

    fwd_copy(0).start()

    @pl.loop(1, members)
    def _(d):
        back_wait(d).wait_recv()
        fwd_copy(d).start()

    @pl.loop(1, members)
    def _(d):
        back_copy(d).wait_send()

    @pl.loop(0, members)
    def _(d):
        fwd_copy(d).wait_send()

    @pl.loop(0, members)
    def _(d):
        there = result.at[1 - core, pl.ds(0, chunk), :]
        pltpu.make_async_remote_copy(
            there, there, fwd_ss.at[d], fwd_rs.at[d], device_id=sibling, device_id_type=MESH
        ).wait_recv()

    k_outs = []
    for k in range(2):
        for half in range(2):
            k_outs.append(
                load(
                    result.at[k, pl.ds(128 * half, 128), :],
                    out_k.at[k, w_rows[half], :],
                    k_out_sem.at[k, half],
                )
            )
    for copy in outs + k_outs:
        copy.wait()


def body(sizes, *arrays):
    ny, nz, rows, width, _ = sizes
    pix = rows * width
    flat = [a.reshape(pix, 128) for a in arrays[:6]]
    weights = [w.reshape(9, 256, 128) for w in arrays[6:8]]
    grads = [a.reshape(pix, 128) for a in arrays[8:]]
    members = 2 * ny
    chunk = 256 // members
    dma = pltpu.SemaphoreType.DMA
    out_c, out_r, out_k = pl.pallas_call(
        functools.partial(kernel, sizes),
        name="interval_back",
        out_shape=(
            jax.ShapeDtypeStruct((pix, 128), F32),
            jax.ShapeDtypeStruct((pix, 128), F32),
            jax.ShapeDtypeStruct((2, 256, 1152), BF16),
        ),
        in_specs=[pl.BlockSpec(memory_space=pl.ANY)] * 10,
        out_specs=(pl.BlockSpec(memory_space=pl.ANY),) * 3,
        scratch_shapes=[
            pltpu.VMEM((2, pix, 128), BF16),
            pltpu.VMEM((2, pix, 128), jnp.int32),
            pltpu.VMEM((2, 256, 1152), BF16),
            pltpu.VMEM((2, 256, 1152), BF16),
            pltpu.VMEM((2, 2, 2, pix, 128), BF16),
            pltpu.VMEM((2, 256, pix), BF16),
            pltpu.VMEM((2, pix, 128), BF16),
            pltpu.VMEM((2, pix, 128), BF16),
            pltpu.VMEM((2, 2, 2, width, 128), BF16),
            pltpu.VMEM((2, pix, 1152), BF16),
            pltpu.VMEM((2, pix, 128), F32),
            pltpu.VMEM((2, 2, pix, 128), BF16),
            pltpu.VMEM((2, 2, pix, 128), BF16),
            pltpu.VMEM((2, pix, 128), F32),
            pltpu.VMEM((2, 256, 1152), F32),
            pltpu.VMEM((256, 1152), BF16),
            pltpu.VMEM((256, 1152), BF16),
            pltpu.VMEM((256, 1152), BF16),
            pltpu.VMEM((members, chunk, 1152), BF16),
            pltpu.VMEM((chunk, 1152), BF16),
            pltpu.VMEM((nz, chunk, 1152), BF16),
            pltpu.VMEM((2, 256, 1152), BF16),
            dma((4,)),
            dma((2,)),
            dma((4,)),
            dma((2, 2)),
            dma((2, 2)),
            dma((2, 2)),
            dma((2, 2)),
            dma((2, 2)),
            dma((2, 2)),
            dma((2,)),
            dma((members - 1,)),
            dma((members - 1,)),
            dma((nz - 1,)),
            dma((nz - 1,)),
            dma((members - 1,)),
            dma((members - 1,)),
            dma((members,)),
            dma((members,)),
            dma((2,)),
            dma((2, 2)),
        ],
        compiler_params=pltpu.CompilerParams(
            collective_id=0, has_side_effects=True, vmem_limit_bytes=48 << 20
        ),
    )(*flat, *weights, *grads)
    kernels = out_k.reshape(2, 256, 9, 128).transpose(0, 2, 1, 3).reshape(2, 3, 3, 256, 128)
    shape = arrays[0].shape
    return out_c.reshape(shape), out_r.reshape(shape), kernels[1], kernels[0]


def solution(mesh):
    wide = P("dp", "slab", None, "chan")
    narrow = P(None, None, None, "chan")
    ny, nz = mesh.shape["dp"] // 2, mesh.shape["slab"] // 2

    def whole(*arrays):
        images, height, width, _ = arrays[0].shape
        sizes = (ny, nz, height // (2 * nz), width, 1.0 / math.sqrt(images * height * width))
        return jax.shard_map(
            functools.partial(body, sizes),
            mesh=mesh,
            in_specs=(wide,) * 6 + (narrow,) * 2 + (wide,) * 2,
            out_specs=(wide, wide, narrow, narrow),
            check_vma=False,
        )(*arrays)

    return whole
```

```python
import functools
import math

import jax
import jax.numpy as jnp
from jax import lax
from jax.experimental import pallas as pl
from jax.experimental.pallas import tpu as pltpu
from jax.sharding import PartitionSpec as P

MESH = pl.DeviceIdType.MESH
F32 = jnp.float32
BF16 = jnp.bfloat16


def relu_back(grad_c, grad_r, states):
    average = 0.5 * (grad_c + grad_r)
    keep_c = jnp.where(states == 1, grad_c, jnp.where(states == 2, average, 0.0))
    keep_r = jnp.where(states == 1, grad_r, jnp.where(states == 2, average, 0.0))
    return keep_c.astype(BF16), keep_r.astype(BF16)


def kernel(
    sizes,
    center_in,
    radius_in,
    hidden_center,
    hidden_radius,
    state_one,
    state_two,
    weight_one,
    weight_two,
    grad_center,
    grad_radius,
    out_c,
    out_r,
    out_k,
    grads,
    states,
    wcat,
    wabs,
    act,
    act_t,
    skip,
    inner,
    halo,
    cols,
    part_own,
    part_send,
    part_recv,
    final,
    k_full,
    k_recv,
    k_mine,
    got_one,
    two,
    got_two,
    result,
    in_sem,
    w_sem,
    act_sem,
    halo_ss,
    halo_rs,
    act_ss,
    act_rs,
    part_ss,
    part_rs,
    core_ss,
    core_rs,
    one_ss,
    one_rs,
    two_ss,
    two_rs,
    back_ss,
    back_rs,
    fwd_ss,
    fwd_rs,
    out_sem,
    k_out_sem,
):
    ny, nz, rows, width, scale = sizes
    pix = rows * width
    dp, slab, chan = lax.axis_index("dp"), lax.axis_index("slab"), lax.axis_index("chan")
    y, core = lax.div(dp, 2), lax.rem(dp, 2)
    z, x_lo = lax.div(slab, 2), lax.rem(slab, 2)
    slabs = 2 * nz
    first = core == 0
    members = 2 * ny
    chunk = 256 // members
    pos_one = jnp.where(first, y, z) * 2 + x_lo
    pos_two = jnp.where(first, z, y)

    def one_dev(j):
        a = lax.div(j, 2)
        return (
            jnp.where(first, a, y) * 2 + core,
            jnp.where(first, z, a) * 2 + lax.rem(j, 2),
            chan,
        )

    def two_dev(j):
        return (jnp.where(first, y, j) * 2 + core, jnp.where(first, j, z) * 2 + x_lo, chan)

    partner = (dp, slab, 1 - chan)
    sibling = (y * 2 + 1 - core, slab, chan)
    above = (dp, lax.rem(slab + slabs - 1, slabs), chan)
    below = (dp, lax.rem(slab + 1, slabs), chan)

    def load(src, dst, sem):
        copy = pltpu.make_async_copy(src, dst, sem)
        copy.start()
        return copy

    c_grad = load(grad_center, grads.at[0], in_sem.at[0])
    r_grad = load(grad_radius, grads.at[1], in_sem.at[1])
    s_two = load(state_two, states.at[1], in_sem.at[2])

    barrier = pltpu.get_barrier_semaphore()
    for peer in (partner, sibling, above, below):
        pl.semaphore_signal(barrier, inc=1, device_id=peer, device_id_type=MESH)

    @pl.loop(1, members)
    def _(d):
        pl.semaphore_signal(
            barrier, inc=1, device_id=one_dev(lax.rem(pos_one + d, members)), device_id_type=MESH
        )

    @pl.loop(1, nz)
    def _(d):
        pl.semaphore_signal(
            barrier, inc=1, device_id=two_dev(lax.rem(pos_two + d, nz)), device_id_type=MESH
        )

    w_rows = (
        pl.ds(pl.multiple_of(chan * 128, 128), 128),
        pl.ds(pl.multiple_of((1 - chan) * 128, 128), 128),
    )

    def load_w(src, layer):
        for tap in range(9):
            for half in range(2):
                pltpu.make_async_copy(
                    src.at[tap, w_rows[half], :],
                    wcat.at[layer, pl.ds(128 * half, 128), pl.ds(128 * tap, 128)],
                    w_sem.at[layer],
                ).start()

    def wait_w(layer):
        pltpu.make_async_copy(wcat.at[layer], wcat.at[layer], w_sem.at[layer]).wait()

    load_w(weight_two, 1)
    acts = ((center_in, radius_in), (hidden_center, hidden_radius))
    act_own = [[load(acts[l][x], act.at[l, x, 0], act_sem.at[2 * l + x]) for x in range(2)] for l in range(2)]
    s_one = load(state_one, states.at[0], in_sem.at[3])
    load_w(weight_one, 0)

    c_grad.wait()
    r_grad.wait()
    s_two.wait()
    for r in range(rows):
        at = pl.ds(r * width, width)
        sc, sr = relu_back(grads[0, at, :].astype(F32), grads[1, at, :].astype(F32), states[1, at, :])
        skip[0, at, :] = sc
        skip[1, at, :] = sr

    column = lax.broadcasted_iota(jnp.int32, (width, 128), 0)

    def place(x, row, value):
        wide = value.astype(F32)
        later = jnp.where(column == width - 1, 0.0, pltpu.roll(wide, width - 1, 0)).astype(BF16)
        sooner = jnp.where(column == 0, 0.0, pltpu.roll(wide, 1, 0)).astype(BF16)
        for a in range(3):
            r = row - 2 + a
            if 0 <= r < rows:
                for b, shifted in enumerate((later, value, sooner)):
                    cols[x, pl.ds(r * width, width), pl.ds(128 * (3 * a + b), 128)] = shifted

    def place_inside(source):
        for x in range(2):
            for r in range(rows):
                place(x, r + 1, source[x, pl.ds(r * width, width), :])

    def send_halo(source, layer):
        up = pltpu.make_async_remote_copy(
            source.at[:, pl.ds(0, width), :], halo.at[layer, 1],
            halo_ss.at[layer, 0], halo_rs.at[layer, 1], device_id=above, device_id_type=MESH,
        )
        down = pltpu.make_async_remote_copy(
            source.at[:, pl.ds((rows - 1) * width, width), :], halo.at[layer, 0],
            halo_ss.at[layer, 1], halo_rs.at[layer, 0], device_id=below, device_id_type=MESH,
        )
        up.start()
        down.start()
        return up, down

    def place_halo(copies, layer):
        copies[0].wait()
        copies[1].wait()
        top = slab > 0
        bottom = slab < slabs - 1
        for x in range(2):
            above_row = halo[layer, 0, x].astype(F32)
            below_row = halo[layer, 1, x].astype(F32)
            place(x, 0, jnp.where(top, above_row, 0.0).astype(BF16))
            place(x, rows + 1, jnp.where(bottom, below_row, 0.0).astype(BF16))

    def send_act(layer):
        copies = []
        for x in range(2):
            copy = pltpu.make_async_remote_copy(
                act.at[layer, x, 0], act.at[layer, x, 1],
                act_ss.at[layer, x], act_rs.at[layer, x], device_id=partner, device_id_type=MESH,
            )
            act_own[layer][x].wait()
            copy.start()
            copies.append(copy)
        return copies

    def convolve(layer):
        copies = []
        for x in range(2):
            weight = wcat[layer] if x == 0 else wabs[layer]
            both = lax.dot_general(
                cols[x], weight, (((1,), (1,)), ((), ())), preferred_element_type=F32
            )
            part_own[x] = both[:, :128]
            part_send[layer, x] = both[:, 128:].astype(BF16)
            copy = pltpu.make_async_remote_copy(
                part_send.at[layer, x], part_recv.at[layer, x],
                part_ss.at[layer, x], part_rs.at[layer, x], device_id=partner, device_id_type=MESH,
            )
            copy.start()
            copies.append(copy)
        return copies

    def turn_own(layer):
        for x in range(2):
            act_t[x, :128, :] = act[layer, x, 0].T

    def kernel_terms(layer, copies):
        for x in range(2):
            copies[x].wait()
            act_t[x, 128:, :] = act[layer, x, 1].T
        for a in range(3):
            at = pl.ds(384 * a, 384)
            kc = jnp.dot(act_t[0], cols[0, :, at], preferred_element_type=F32)
            kr = jnp.dot(act_t[1], cols[1, :, at], preferred_element_type=F32)
            w = wcat[layer, :, at].astype(F32)
            kr = jnp.where(w > 0.0, kr, jnp.where(w < 0.0, -kr, 0.0))
            k_full[layer, :, at] = scale * (kc + kr)

    def own_cols(which):
        return pl.ds(pl.multiple_of(which * 512, 512), 640)

    def rows_of(j):
        return pl.ds(pl.multiple_of(j * chunk, chunk), chunk)

    def far_first(i, count):
        k = lax.div(i + 1, 2)
        return count // 2 + jnp.where(lax.rem(i, 2) == 1, k, -k)

    def core_copy(layer):
        return pltpu.make_async_remote_copy(
            k_full.at[layer, :, own_cols(1 - core)], k_recv.at[layer],
            core_ss.at[layer], core_rs.at[layer], device_id=sibling, device_id_type=MESH,
        )

    def one_copy(layer, d):
        j = lax.rem(pos_one + d, members)
        return pltpu.make_async_remote_copy(
            k_mine.at[layer, rows_of(j), :], got_one.at[layer, pos_one],
            one_ss.at[layer, d - 1], one_rs.at[layer, d - 1],
            device_id=one_dev(j), device_id_type=MESH,
        )

    def two_copy(layer, d):
        return pltpu.make_async_remote_copy(
            two.at[layer], got_two.at[layer, pos_two],
            two_ss.at[layer, d - 1], two_rs.at[layer, d - 1],
            device_id=two_dev(lax.rem(pos_two + d, nz)), device_id_type=MESH,
        )

    def back_copy(layer, d):
        j = lax.rem(pos_one + d, members)
        mine = result.at[layer, core, rows_of(pos_one), :]
        return pltpu.make_async_remote_copy(
            mine, mine, back_ss.at[layer, d - 1], back_rs.at[layer, d - 1],
            device_id=one_dev(j), device_id_type=MESH,
        )

    def back_from(layer, d):
        there = result.at[layer, core, rows_of(lax.rem(pos_one - d + members, members)), :]
        return pltpu.make_async_remote_copy(
            there, there, back_ss.at[layer, d - 1], back_rs.at[layer, d - 1],
            device_id=sibling, device_id_type=MESH,
        )

    def fwd_copy(layer, d):
        there = result.at[layer, core, rows_of(lax.rem(pos_one - d + members, members)), :]
        return pltpu.make_async_remote_copy(
            there, there, fwd_ss.at[layer, d], fwd_rs.at[layer, d],
            device_id=sibling, device_id_type=MESH,
        )

    def fwd_from(layer, d):
        there = result.at[layer, 1 - core, pl.ds(0, chunk), :]
        return pltpu.make_async_remote_copy(
            there, there, fwd_ss.at[layer, d], fwd_rs.at[layer, d],
            device_id=sibling, device_id_type=MESH,
        )

    def scatter(layer):
        core_copy(layer).wait()
        own = k_full[layer, :, own_cols(core)]
        k_mine[layer] = (own + k_recv[layer]).astype(BF16)

        @pl.loop(0, members - 1)
        def _(i):
            one_copy(layer, far_first(i, members)).start()

        got_one[layer, pos_one] = k_mine[layer, rows_of(pos_one), :]

    def spread(layer):
        @pl.loop(1, members)
        def _(d):
            one_copy(layer, d).wait()

        total = got_one[layer, 0].astype(F32)
        for j in range(1, members):
            total = total + got_one[layer, j].astype(F32)
        two[layer] = total.astype(BF16)

        @pl.loop(0, nz - 1)
        def _(i):
            two_copy(layer, far_first(i, nz)).start()

        got_two[layer, pos_two] = two[layer]

    def gather(layer):
        @pl.loop(1, nz)
        def _(d):
            two_copy(layer, d).wait()

        total = got_two[layer, 0].astype(F32)
        for j in range(1, nz):
            total = total + got_two[layer, j].astype(F32)
        result[layer, core, rows_of(pos_one), :] = total.astype(BF16)

        @pl.loop(0, members - 1)
        def _(i):
            back_copy(layer, far_first(i, members)).start()

        fwd_copy(layer, 0).start()

    def write_out(layer, which):
        for tap in range(0, 5) if which == 0 else range(5, 9):
            for half in range(2):
                pltpu.make_async_copy(
                    result.at[layer, which, pl.ds(128 * half, 128), pl.ds(128 * (tap - 4 * which), 128)],
                    out_k.at[layer, tap, w_rows[half], :],
                    k_out_sem.at[layer],
                ).start()

    def deliver(layer):
        @pl.loop(1, members)
        def _(d):
            back_from(layer, d).wait_recv()
            fwd_copy(layer, d).start()

        @pl.loop(0, members)
        def _(d):
            fwd_from(layer, d).wait_recv()

        write_out(layer, 0)
        write_out(layer, 1)

        @pl.loop(1, members)
        def _(d):
            back_copy(layer, d).wait_send()

        @pl.loop(0, members)
        def _(d):
            fwd_copy(layer, d).wait_send()

    place_inside(skip)
    pl.semaphore_wait(barrier, 4 + members - 1 + nz - 1)
    halo_two = send_halo(skip, 1)
    act_two = send_act(1)
    wait_w(1)
    wabs[1] = jnp.abs(wcat[1])
    turn_own(1)
    place_halo(halo_two, 1)
    part_two = convolve(1)
    act_one = send_act(0)

    kernel_terms(1, act_two)
    core_copy(1).start()
    turn_own(0)
    wait_w(0)
    wabs[0] = jnp.abs(wcat[0])
    s_one.wait()
    scatter(1)

    for copy in part_two:
        copy.wait()
    for r in range(rows):
        at = pl.ds(r * width, width)
        back_c = part_own[0, at, :] + part_recv[1, 0, at, :].astype(F32)
        back_r = part_own[1, at, :] + part_recv[1, 1, at, :].astype(F32)
        ic, ir = relu_back(back_c, back_r, states[0, at, :])
        inner[0, at, :] = ic
        inner[1, at, :] = ir
    halo_one = send_halo(inner, 0)
    place_inside(inner)
    place_halo(halo_one, 0)

    kernel_terms(0, act_one)
    core_copy(0).start()
    spread(1)
    scatter(0)
    part_one = convolve(0)
    gather(1)
    spread(0)

    outs = []
    for x, out in enumerate((out_c, out_r)):
        part_one[x].wait()
        final[x] = skip[x].astype(F32) + part_own[x] + part_recv[0, x].astype(F32)
        outs.append(load(final.at[x], out, out_sem.at[x]))
    deliver(1)
    gather(0)
    deliver(0)
    for copy in outs:
        copy.wait()
    for layer in range(2):
        pltpu.make_async_copy(out_k.at[layer], out_k.at[layer], k_out_sem.at[layer]).wait()


def hand_over(made_c, made_r, made_k, out_c, out_r, out_one, out_two, wide, taps, load_sem, sem):
    sources = (made_c, made_r, made_k.at[0], made_k.at[1])
    buffers = (wide.at[0], wide.at[1], taps.at[0], taps.at[1])
    targets = (out_c, out_r, out_one, out_two)
    loads = []
    stores = []
    for i in range(4):
        loads.append(pltpu.make_async_copy(sources[i], buffers[i], load_sem.at[i]))
        stores.append(pltpu.make_async_copy(buffers[i], targets[i], sem.at[i]))
    for copy in loads:
        copy.start()
    for i in range(4):
        loads[i].wait()
        stores[i].start()
    for copy in stores:
        copy.wait()


def body(sizes, *arrays):
    ny, nz, rows, width, _ = sizes
    pix = rows * width
    flat = [a.reshape(pix, 128) for a in arrays[:6]]
    weights = [w.reshape(9, 256, 128) for w in arrays[6:8]]
    grads = [a.reshape(pix, 128) for a in arrays[8:]]
    members = 2 * ny
    chunk = 256 // members
    dma = pltpu.SemaphoreType.DMA
    out_c, out_r, out_k = pl.pallas_call(
        functools.partial(kernel, sizes),
        name="interval_back",
        out_shape=(
            jax.ShapeDtypeStruct((pix, 128), F32),
            jax.ShapeDtypeStruct((pix, 128), F32),
            jax.ShapeDtypeStruct((2, 9, 256, 128), BF16),
        ),
        in_specs=[pl.BlockSpec(memory_space=pl.ANY)] * 10,
        out_specs=(pl.BlockSpec(memory_space=pl.ANY),) * 3,
        scratch_shapes=[
            pltpu.VMEM((2, pix, 128), BF16),
            pltpu.VMEM((2, pix, 128), jnp.int32),
            pltpu.VMEM((2, 256, 1152), BF16),
            pltpu.VMEM((2, 256, 1152), BF16),
            pltpu.VMEM((2, 2, 2, pix, 128), BF16),
            pltpu.VMEM((2, 256, pix), BF16),
            pltpu.VMEM((2, pix, 128), BF16),
            pltpu.VMEM((2, pix, 128), BF16),
            pltpu.VMEM((2, 2, 2, width, 128), BF16),
            pltpu.VMEM((2, pix, 1152), BF16),
            pltpu.VMEM((2, pix, 128), F32),
            pltpu.VMEM((2, 2, pix, 128), BF16),
            pltpu.VMEM((2, 2, pix, 128), BF16),
            pltpu.VMEM((2, pix, 128), F32),
            pltpu.VMEM((2, 256, 1152), F32),
            pltpu.VMEM((2, 256, 640), F32),
            pltpu.VMEM((2, 256, 640), BF16),
            pltpu.VMEM((2, members, chunk, 640), BF16),
            pltpu.VMEM((2, chunk, 640), BF16),
            pltpu.VMEM((2, nz, chunk, 640), BF16),
            pltpu.VMEM((2, 2, 256, 640), BF16),
            dma((4,)),
            dma((2,)),
            dma((4,)),
            dma((2, 2)),
            dma((2, 2)),
            dma((2, 2)),
            dma((2, 2)),
            dma((2, 2)),
            dma((2, 2)),
            dma((2,)),
            dma((2,)),
            dma((2, members - 1)),
            dma((2, members - 1)),
            dma((2, nz - 1)),
            dma((2, nz - 1)),
            dma((2, members - 1)),
            dma((2, members - 1)),
            dma((2, members)),
            dma((2, members)),
            dma((2,)),
            dma((2,)),
        ],
        compiler_params=pltpu.CompilerParams(
            collective_id=0, has_side_effects=True, vmem_limit_bytes=62 << 20
        ),
    )(*flat, *weights, *grads)
    shape = arrays[0].shape
    out_c, out_r, k_one, k_two = pl.pallas_call(
        hand_over,
        name="hand_over",
        out_shape=(
            jax.ShapeDtypeStruct((pix, 128), F32),
            jax.ShapeDtypeStruct((pix, 128), F32),
            jax.ShapeDtypeStruct((9, 256, 128), BF16),
            jax.ShapeDtypeStruct((9, 256, 128), BF16),
        ),
        in_specs=[pl.BlockSpec(memory_space=pl.ANY)] * 3,
        out_specs=(pl.BlockSpec(memory_space=pl.ANY),) * 4,
        scratch_shapes=[
            pltpu.VMEM((2, pix, 128), F32),
            pltpu.VMEM((2, 9, 256, 128), BF16),
            dma((4,)),
            dma((4,)),
        ],
        compiler_params=pltpu.CompilerParams(vmem_limit_bytes=62 << 20),
    )(out_c, out_r, out_k)
    taps = (3, 3, 256, 128)
    return out_c.reshape(shape), out_r.reshape(shape), k_one.reshape(taps), k_two.reshape(taps)


def solution(mesh):
    wide = P("dp", "slab", None, "chan")
    narrow = P(None, None, None, "chan")
    ny, nz = mesh.shape["dp"] // 2, mesh.shape["slab"] // 2

    def whole(*arrays):
        images, height, width, _ = arrays[0].shape
        sizes = (ny, nz, height // (2 * nz), width, 1.0 / math.sqrt(images * height * width))
        return jax.shard_map(
            functools.partial(body, sizes),
            mesh=mesh,
            in_specs=(wide,) * 6 + (narrow,) * 2 + (wide,) * 2,
            out_specs=(wide, wide, narrow, narrow),
            check_vma=False,
        )(*arrays)

    return whole
```

```python
import functools
import math

import jax
import jax.numpy as jnp
from jax import lax
from jax.experimental import pallas as pl
from jax.experimental.pallas import tpu as pltpu
from jax.sharding import PartitionSpec as P

MESH = pl.DeviceIdType.MESH
F32 = jnp.float32
BF16 = jnp.bfloat16


def relu_back(grad_c, grad_r, states):
    average = 0.5 * (grad_c + grad_r)
    keep_c = jnp.where(states == 1, grad_c, jnp.where(states == 2, average, 0.0))
    keep_r = jnp.where(states == 1, grad_r, jnp.where(states == 2, average, 0.0))
    return keep_c.astype(BF16), keep_r.astype(BF16)


def kernel(
    sizes,
    center_in,
    radius_in,
    hidden_center,
    hidden_radius,
    state_one,
    state_two,
    weight_one,
    weight_two,
    grad_center,
    grad_radius,
    out_c,
    out_r,
    out_k,
    grads,
    states,
    wcat,
    wabs,
    act,
    act_t,
    skip,
    inner,
    halo,
    cols,
    part_own,
    part_send,
    part_recv,
    final,
    k_full,
    k_recv,
    k_mine,
    got_one,
    two,
    got_two,
    result,
    in_sem,
    w_sem,
    act_sem,
    halo_ss,
    halo_rs,
    act_ss,
    act_rs,
    part_ss,
    part_rs,
    core_ss,
    core_rs,
    one_ss,
    one_rs,
    two_ss,
    two_rs,
    back_ss,
    back_rs,
    fwd_ss,
    fwd_rs,
    out_sem,
    k_out_sem,
):
    ny, nz, rows, width, scale = sizes
    pix = rows * width
    dp, slab, chan = lax.axis_index("dp"), lax.axis_index("slab"), lax.axis_index("chan")
    y, core = lax.div(dp, 2), lax.rem(dp, 2)
    z, x_lo = lax.div(slab, 2), lax.rem(slab, 2)
    slabs = 2 * nz
    first = core == 0
    members = 2 * ny
    chunk = 256 // members
    pos_one = jnp.where(first, y, z) * 2 + x_lo
    pos_two = jnp.where(first, z, y)

    def one_dev(j):
        a, x = lax.div(j, 2), lax.rem(j, 2)
        return (jnp.where(first, a, y) * 2 + core, jnp.where(first, z, a) * 2 + x, chan)

    def two_dev(j):
        return (jnp.where(first, y, j) * 2 + core, jnp.where(first, j, z) * 2 + x_lo, chan)

    partner = (dp, slab, 1 - chan)
    sibling = (y * 2 + 1 - core, slab, chan)
    above = (dp, lax.rem(slab + slabs - 1, slabs), chan)
    below = (dp, lax.rem(slab + 1, slabs), chan)

    def load(src, dst, sem):
        copy = pltpu.make_async_copy(src, dst, sem)
        copy.start()
        return copy

    c_grad = load(grad_center, grads.at[0], in_sem.at[0])
    r_grad = load(grad_radius, grads.at[1], in_sem.at[1])
    s_two = load(state_two, states.at[1], in_sem.at[2])

    def far_first(i, count):
        k = lax.div(i + 1, 2)
        return count // 2 + jnp.where(lax.rem(i, 2) == 1, k, -k)

    barrier = pltpu.get_barrier_semaphore()

    @pl.loop(0, members - 1)
    def _(i):
        d = far_first(i, members)
        peer = one_dev(lax.rem(pos_one + d, members))
        pl.semaphore_signal(barrier, inc=1, device_id=peer, device_id_type=MESH)

    @pl.loop(0, nz - 1)
    def _(i):
        peer = two_dev(lax.rem(pos_two + far_first(i, nz), nz))
        pl.semaphore_signal(barrier, inc=1, device_id=peer, device_id_type=MESH)

    for peer in (partner, above, below, sibling):
        pl.semaphore_signal(barrier, inc=1, device_id=peer, device_id_type=MESH)

    own_at = pl.ds(pl.multiple_of(chan * 128, 128), 128)
    other_at = pl.ds(pl.multiple_of((1 - chan) * 128, 128), 128)
    lower = chan == 0

    def load_w(src, layer):
        for tap in range(9):
            pltpu.make_async_copy(
                src.at[tap], wcat.at[layer, :, pl.ds(128 * tap, 128)], w_sem.at[layer]
            ).start()

    def wait_w(layer):
        pltpu.make_async_copy(wcat.at[layer], wcat.at[layer], w_sem.at[layer]).wait()

    acts = ((center_in, radius_in), (hidden_center, hidden_radius))
    act_own = [[load(acts[l][x], act.at[l, x, 0], act_sem.at[2 * l + x]) for x in range(2)] for l in range(2)]
    s_one = load(state_one, states.at[0], in_sem.at[3])

    c_grad.wait()
    r_grad.wait()
    s_two.wait()
    for r in (0, rows - 1, *range(1, rows - 1)):
        at = pl.ds(r * width, width)
        sc, sr = relu_back(grads[0, at, :].astype(F32), grads[1, at, :].astype(F32), states[1, at, :])
        skip[0, at, :] = sc
        skip[1, at, :] = sr

    column = lax.broadcasted_iota(jnp.int32, (width, 128), 0)

    def place(layer, x, row, value):
        wide = value.astype(F32)
        later = jnp.where(column == width - 1, 0.0, pltpu.roll(wide, width - 1, 0)).astype(BF16)
        sooner = jnp.where(column == 0, 0.0, pltpu.roll(wide, 1, 0)).astype(BF16)
        for a in range(3):
            r = row - 2 + a
            if 0 <= r < rows:
                for b, shifted in enumerate((later, value, sooner)):
                    cols[layer, x, pl.ds(r * width, width), pl.ds(128 * (3 * a + b), 128)] = shifted

    def place_inside(source, layer):
        for x in range(2):
            for r in range(rows):
                place(layer, x, r + 1, source[x, pl.ds(r * width, width), :])

    def send_halo(source, layer):
        up = pltpu.make_async_remote_copy(
            source.at[:, pl.ds(0, width), :], halo.at[layer, 1],
            halo_ss.at[layer, 0], halo_rs.at[layer, 1], device_id=above, device_id_type=MESH,
        )
        down = pltpu.make_async_remote_copy(
            source.at[:, pl.ds((rows - 1) * width, width), :], halo.at[layer, 0],
            halo_ss.at[layer, 1], halo_rs.at[layer, 0], device_id=below, device_id_type=MESH,
        )
        up.start()
        down.start()
        return up, down

    def place_halo(copies, layer):
        copies[0].wait()
        copies[1].wait()
        top = slab > 0
        bottom = slab < slabs - 1
        for x in range(2):
            above_row = halo[layer, 0, x].astype(F32)
            below_row = halo[layer, 1, x].astype(F32)
            place(layer, x, 0, jnp.where(top, above_row, 0.0).astype(BF16))
            place(layer, x, rows + 1, jnp.where(bottom, below_row, 0.0).astype(BF16))

    def send_act(layer, x):
        copy = pltpu.make_async_remote_copy(
            act.at[layer, x, 0], act.at[layer, x, 1],
            act_ss.at[layer, x], act_rs.at[layer, x], device_id=partner, device_id_type=MESH,
        )
        act_own[layer][x].wait()
        copy.start()
        return copy

    def convolve(layer):
        copies = []
        for x in range(2):
            weight = wcat[layer] if x == 0 else wabs[layer]
            both = lax.dot_general(
                cols[layer, x], weight, (((1,), (1,)), ((), ())), preferred_element_type=F32
            )
            part_own[x] = jnp.where(lower, both[:, :128], both[:, 128:])
            part_send[layer, x] = jnp.where(lower, both[:, 128:], both[:, :128]).astype(BF16)
            copy = pltpu.make_async_remote_copy(
                part_send.at[layer, x], part_recv.at[layer, x],
                part_ss.at[layer, x], part_rs.at[layer, x], device_id=partner, device_id_type=MESH,
            )
            if layer == 1:
                copy.start()
            copies.append(copy)
        return copies

    def turn_own(layer):
        for x in range(2):
            act_t[layer, x, own_at, :] = act[layer, x, 0].T

    def kernel_terms(layer, copies):
        for x in range(2):
            copies[x].wait()
            act_t[layer, x, other_at, :] = act[layer, x, 1].T
        for i in range(3):
            a = jnp.where(first, 2 - i, i)
            at = pl.ds(pl.multiple_of(384 * a, 128), 384)
            kc = jnp.dot(act_t[layer, 0], cols[layer, 0, :, at], preferred_element_type=F32)
            kr = jnp.dot(act_t[layer, 1], cols[layer, 1, :, at], preferred_element_type=F32)
            w = wcat[layer, :, at].astype(F32)
            kr = jnp.where(w > 0.0, kr, jnp.where(w < 0.0, -kr, 0.0))
            k_full[layer, :, at] = scale * (kc + kr)
            if i < 2:
                core_copy(layer, i).start()

    def own_cols(which):
        return pl.ds(pl.multiple_of(which * 512, 512), 640)

    def rows_of(j):
        return pl.ds(pl.multiple_of(j * chunk, chunk), chunk)

    def core_copy(layer, i):
        size = (384, 256)[i]
        src = jnp.where(first, (768, 512)[i], (0, 384)[i])
        dst = jnp.where(first, (256, 0)[i], (0, 384)[i])
        return pltpu.make_async_remote_copy(
            k_full.at[layer, :, pl.ds(pl.multiple_of(src, 128), size)],
            k_recv.at[layer, :, pl.ds(pl.multiple_of(dst, 128), size)],
            core_ss.at[layer, i], core_rs.at[layer, i], device_id=sibling, device_id_type=MESH,
        )

    def one_copy(layer, d):
        j = lax.rem(pos_one + d, members)
        return pltpu.make_async_remote_copy(
            k_mine.at[layer, rows_of(j), :], got_one.at[layer, pos_one],
            one_ss.at[layer, d - 1], one_rs.at[layer, d - 1],
            device_id=one_dev(j), device_id_type=MESH,
        )

    def two_copy(layer, d):
        return pltpu.make_async_remote_copy(
            two.at[layer], got_two.at[layer, pos_two],
            two_ss.at[layer, d - 1], two_rs.at[layer, d - 1],
            device_id=two_dev(lax.rem(pos_two + d, nz)), device_id_type=MESH,
        )

    def back_copy(layer, d):
        j = lax.rem(pos_one + d, members)
        mine = result.at[layer, core, rows_of(pos_one), :]
        return pltpu.make_async_remote_copy(
            mine, mine, back_ss.at[layer, d - 1], back_rs.at[layer, d - 1],
            device_id=one_dev(j), device_id_type=MESH,
        )

    def landed(layer, d):
        j = lax.rem(pos_one - d + members, members)
        return result.at[layer, core, rows_of(j), :]

    def back_from(layer, d):
        there = landed(layer, d)
        return pltpu.make_async_remote_copy(
            there, there, back_ss.at[layer, d - 1], back_rs.at[layer, d - 1],
            device_id=sibling, device_id_type=MESH,
        )

    def fwd_copy(layer, d):
        there = landed(layer, d)
        return pltpu.make_async_remote_copy(
            there, there, fwd_ss.at[layer, d], fwd_rs.at[layer, d],
            device_id=sibling, device_id_type=MESH,
        )

    def fwd_from(layer, d):
        there = result.at[layer, 1 - core, pl.ds(0, chunk), :]
        return pltpu.make_async_remote_copy(
            there, there, fwd_ss.at[layer, d], fwd_rs.at[layer, d],
            device_id=sibling, device_id_type=MESH,
        )

    def scatter(layer):
        for i in range(2):
            core_copy(layer, i).wait()
        own = k_full[layer, :, own_cols(core)]
        k_mine[layer] = (own + k_recv[layer]).astype(BF16)

        @pl.loop(0, members - 1)
        def _(i):
            one_copy(layer, far_first(i, members)).start()

        got_one[layer, pos_one] = k_mine[layer, rows_of(pos_one), :]

    def spread(layer):
        @pl.loop(1, members)
        def _(d):
            one_copy(layer, d).wait()

        total = got_one[layer, 0].astype(F32)
        for j in range(1, members):
            total = total + got_one[layer, j].astype(F32)
        two[layer] = total.astype(BF16)

        @pl.loop(0, nz - 1)
        def _(i):
            two_copy(layer, far_first(i, nz)).start()

        got_two[layer, pos_two] = two[layer]

    def gather(layer):
        @pl.loop(1, nz)
        def _(d):
            two_copy(layer, d).wait()

        total = got_two[layer, 0].astype(F32)
        for j in range(1, nz):
            total = total + got_two[layer, j].astype(F32)
        result[layer, core, rows_of(pos_one), :] = total.astype(BF16)

        @pl.loop(0, members - 1)
        def _(i):
            back_copy(layer, far_first(i, members)).start()

        fwd_copy(layer, 0).start()

    def write_out(layer, which):
        for tap in range(0, 5) if which == 0 else range(5, 9):
            pltpu.make_async_copy(
                result.at[layer, which, :, pl.ds(128 * (tap - 4 * which), 128)],
                out_k.at[layer, tap],
                k_out_sem.at[layer],
            ).start()

    def deliver(layer):
        @pl.loop(1, members)
        def _(d):
            back_from(layer, d).wait_recv()
            fwd_copy(layer, d).start()

        @pl.loop(0, members)
        def _(d):
            fwd_from(layer, d).wait_recv()

        write_out(layer, 0)
        write_out(layer, 1)

        @pl.loop(1, members)
        def _(d):
            back_copy(layer, d).wait_send()

        @pl.loop(0, members)
        def _(d):
            fwd_copy(layer, d).wait_send()

    pl.semaphore_wait(barrier, 4 + members - 1 + nz - 1)
    halo_two = send_halo(skip, 1)
    act_one_c = send_act(0, 0)
    load_w(weight_two, 1)
    place_inside(skip, 1)
    load_w(weight_one, 0)
    wait_w(1)
    wabs[1] = jnp.abs(wcat[1])
    place_halo(halo_two, 1)
    part_two = convolve(1)
    act_one = (act_one_c, send_act(0, 1))
    turn_own(0)
    wait_w(0)
    wabs[0] = jnp.abs(wcat[0])
    s_one.wait()

    for copy in part_two:
        copy.wait()
    for r in range(rows):
        at = pl.ds(r * width, width)
        back_c = part_own[0, at, :] + part_recv[1, 0, at, :].astype(F32)
        back_r = part_own[1, at, :] + part_recv[1, 1, at, :].astype(F32)
        ic, ir = relu_back(back_c, back_r, states[0, at, :])
        inner[0, at, :] = ic
        inner[1, at, :] = ir
    halo_one = send_halo(inner, 0)
    act_two = (send_act(1, 0), send_act(1, 1))
    place_inside(inner, 0)
    turn_own(1)
    place_halo(halo_one, 0)

    kernel_terms(0, act_one)
    scatter(0)

    part_one = convolve(0)

    kernel_terms(1, act_two)
    scatter(1)
    spread(0)
    for copy in part_one:
        copy.start()
    spread(1)
    gather(0)
    gather(1)

    outs = []
    for x, out in enumerate((out_c, out_r)):
        part_one[x].wait()
        final[x] = skip[x].astype(F32) + part_own[x] + part_recv[0, x].astype(F32)
        outs.append(load(final.at[x], out, out_sem.at[x]))
    deliver(0)
    deliver(1)
    for copy in outs:
        copy.wait()
    for layer in range(2):
        pltpu.make_async_copy(out_k.at[layer], out_k.at[layer], k_out_sem.at[layer]).wait()


def hand_over(made_c, made_r, made_k, out_c, out_r, out_one, out_two, wide, taps, load_sem, sem):
    sources = (made_c, made_r, made_k.at[0], made_k.at[1])
    buffers = (wide.at[0], wide.at[1], taps.at[0], taps.at[1])
    targets = (out_c, out_r, out_one, out_two)
    loads = []
    stores = []
    for i in range(4):
        loads.append(pltpu.make_async_copy(sources[i], buffers[i], load_sem.at[i]))
        stores.append(pltpu.make_async_copy(buffers[i], targets[i], sem.at[i]))
    for copy in loads:
        copy.start()
    for i in range(4):
        loads[i].wait()
        stores[i].start()
    for copy in stores:
        copy.wait()


def body(sizes, *arrays):
    ny, nz, rows, width, _ = sizes
    pix = rows * width
    flat = [a.reshape(pix, 128) for a in arrays[:6]]
    weights = [w.reshape(9, 256, 128) for w in arrays[6:8]]
    grads = [a.reshape(pix, 128) for a in arrays[8:]]
    dma = pltpu.SemaphoreType.DMA
    out_c, out_r, out_k = pl.pallas_call(
        functools.partial(kernel, sizes),
        name="interval_back",
        out_shape=(
            jax.ShapeDtypeStruct((pix, 128), F32),
            jax.ShapeDtypeStruct((pix, 128), F32),
            jax.ShapeDtypeStruct((2, 9, 256, 128), BF16),
        ),
        in_specs=[pl.BlockSpec(memory_space=pl.ANY)] * 10,
        out_specs=(pl.BlockSpec(memory_space=pl.ANY),) * 3,
        scratch_shapes=[
            pltpu.VMEM((2, pix, 128), BF16),
            pltpu.VMEM((2, pix, 128), jnp.int32),
            pltpu.VMEM((2, 256, 1152), BF16),
            pltpu.VMEM((2, 256, 1152), BF16),
            pltpu.VMEM((2, 2, 2, pix, 128), BF16),
            pltpu.VMEM((2, 2, 256, pix), BF16),
            pltpu.VMEM((2, pix, 128), BF16),
            pltpu.VMEM((2, pix, 128), BF16),
            pltpu.VMEM((2, 2, 2, width, 128), BF16),
            pltpu.VMEM((2, 2, pix, 1152), BF16),
            pltpu.VMEM((2, pix, 128), F32),
            pltpu.VMEM((2, 2, pix, 128), BF16),
            pltpu.VMEM((2, 2, pix, 128), BF16),
            pltpu.VMEM((2, pix, 128), F32),
            pltpu.VMEM((2, 256, 1152), F32),
            pltpu.VMEM((2, 256, 640), F32),
            pltpu.VMEM((2, 256, 640), BF16),
            pltpu.VMEM((2, 2 * ny, 128 // ny, 640), BF16),
            pltpu.VMEM((2, 128 // ny, 640), BF16),
            pltpu.VMEM((2, nz, 128 // ny, 640), BF16),
            pltpu.VMEM((2, 2, 256, 640), BF16),
            dma((4,)),
            dma((2,)),
            dma((4,)),
            dma((2, 2)),
            dma((2, 2)),
            dma((2, 2)),
            dma((2, 2)),
            dma((2, 2)),
            dma((2, 2)),
            dma((2, 2)),
            dma((2, 2)),
            dma((2, 2 * ny - 1)),
            dma((2, 2 * ny - 1)),
            dma((2, nz - 1)),
            dma((2, nz - 1)),
            dma((2, 2 * ny - 1)),
            dma((2, 2 * ny - 1)),
            dma((2, 2 * ny)),
            dma((2, 2 * ny)),
            dma((2,)),
            dma((2,)),
        ],
        compiler_params=pltpu.CompilerParams(
            collective_id=0, has_side_effects=True, vmem_limit_bytes=62 << 20
        ),
    )(*flat, *weights, *grads)
    shape = arrays[0].shape
    out_c, out_r, k_one, k_two = pl.pallas_call(
        hand_over,
        name="hand_over",
        out_shape=(
            jax.ShapeDtypeStruct((pix, 128), F32),
            jax.ShapeDtypeStruct((pix, 128), F32),
            jax.ShapeDtypeStruct((9, 256, 128), BF16),
            jax.ShapeDtypeStruct((9, 256, 128), BF16),
        ),
        in_specs=[pl.BlockSpec(memory_space=pl.ANY)] * 3,
        out_specs=(pl.BlockSpec(memory_space=pl.ANY),) * 4,
        scratch_shapes=[
            pltpu.VMEM((2, pix, 128), F32),
            pltpu.VMEM((2, 9, 256, 128), BF16),
            dma((4,)),
            dma((4,)),
        ],
        compiler_params=pltpu.CompilerParams(vmem_limit_bytes=62 << 20),
    )(out_c, out_r, out_k)
    taps = (3, 3, 256, 128)
    return out_c.reshape(shape), out_r.reshape(shape), k_one.reshape(taps), k_two.reshape(taps)


def solution(mesh):
    wide = P("dp", "slab", None, "chan")
    narrow = P(None, None, None, "chan")
    ny, nz = mesh.shape["dp"] // 2, mesh.shape["slab"] // 2

    def whole(*arrays):
        images, height, width, _ = arrays[0].shape
        sizes = (ny, nz, height // (2 * nz), width, 1.0 / math.sqrt(images * height * width))
        return jax.shard_map(
            functools.partial(body, sizes),
            mesh=mesh,
            in_specs=(wide,) * 6 + (narrow,) * 2 + (wide,) * 2,
            out_specs=(wide, wide, narrow, narrow),
            check_vma=False,
        )(*arrays)

    return whole
```

```python
import functools
import math

import jax
import jax.numpy as jnp
from jax import lax
from jax.experimental import pallas as pl
from jax.experimental.pallas import tpu as pltpu
from jax.sharding import PartitionSpec as P

MESH = pl.DeviceIdType.MESH
F32 = jnp.float32
BF16 = jnp.bfloat16


def relu_back(grad_c, grad_r, states):
    average = 0.5 * (grad_c + grad_r)
    keep_c = jnp.where(states == 1, grad_c, jnp.where(states == 2, average, 0.0))
    keep_r = jnp.where(states == 1, grad_r, jnp.where(states == 2, average, 0.0))
    return keep_c.astype(BF16), keep_r.astype(BF16)


def kernel(
    sizes,
    center_in,
    radius_in,
    hidden_center,
    hidden_radius,
    state_one,
    state_two,
    weight_one,
    weight_two,
    grad_center,
    grad_radius,
    out_c,
    out_r,
    out_k,
    grads,
    states,
    wcat,
    wabs,
    act,
    act_t,
    skip,
    inner,
    halo,
    cols,
    part_own,
    part_send,
    part_recv,
    final,
    k_full,
    k_recv,
    k_mine,
    got_one,
    two,
    got_two,
    result,
    in_sem,
    w_sem,
    act_sem,
    halo_ss,
    halo_rs,
    act_ss,
    act_rs,
    part_ss,
    part_rs,
    core_ss,
    core_rs,
    one_ss,
    one_rs,
    two_ss,
    two_rs,
    back_ss,
    back_rs,
    fwd_ss,
    fwd_rs,
    out_sem,
    k_out_sem,
):
    ny, nz, rows, width, scale = sizes
    pix = rows * width
    dp, slab, chan = lax.axis_index("dp"), lax.axis_index("slab"), lax.axis_index("chan")
    y, core = lax.div(dp, 2), lax.rem(dp, 2)
    z, x_lo = lax.div(slab, 2), lax.rem(slab, 2)
    slabs = 2 * nz
    first = core == 0
    members = 2 * ny
    chunk = 256 // members
    pos_one = jnp.where(first, y, z) * 2 + x_lo
    pos_two = jnp.where(first, z, y)

    def one_dev(j):
        a, x = lax.div(j, 2), lax.rem(j, 2)
        return (jnp.where(first, a, y) * 2 + core, jnp.where(first, z, a) * 2 + x, chan)

    def two_dev(j):
        return (jnp.where(first, y, j) * 2 + core, jnp.where(first, j, z) * 2 + x_lo, chan)

    partner = (dp, slab, 1 - chan)
    sibling = (y * 2 + 1 - core, slab, chan)
    above = (dp, lax.rem(slab + slabs - 1, slabs), chan)
    below = (dp, lax.rem(slab + 1, slabs), chan)

    def load(src, dst, sem):
        copy = pltpu.make_async_copy(src, dst, sem)
        copy.start()
        return copy

    c_grad = load(grad_center, grads.at[0], in_sem.at[0])
    r_grad = load(grad_radius, grads.at[1], in_sem.at[1])
    s_two = load(state_two, states.at[1], in_sem.at[2])

    def far_first(i, count):
        k = lax.div(i + 1, 2)
        return count // 2 + jnp.where(lax.rem(i, 2) == 1, k, -k)

    barrier = pltpu.get_barrier_semaphore()

    @pl.loop(0, members - 1)
    def _(i):
        d = far_first(i, members)
        peer = one_dev(lax.rem(pos_one + d, members))
        pl.semaphore_signal(barrier, inc=1, device_id=peer, device_id_type=MESH)

    @pl.loop(0, nz - 1)
    def _(i):
        peer = two_dev(lax.rem(pos_two + far_first(i, nz), nz))
        pl.semaphore_signal(barrier, inc=1, device_id=peer, device_id_type=MESH)

    for peer in (partner, above, below, sibling):
        pl.semaphore_signal(barrier, inc=1, device_id=peer, device_id_type=MESH)

    own_at = pl.ds(pl.multiple_of(chan * 128, 128), 128)
    other_at = pl.ds(pl.multiple_of((1 - chan) * 128, 128), 128)
    lower = chan == 0

    def load_w(src, layer):
        for tap in range(9):
            pltpu.make_async_copy(
                src.at[tap], wcat.at[layer, :, pl.ds(128 * tap, 128)], w_sem.at[layer]
            ).start()

    def wait_w(layer):
        pltpu.make_async_copy(wcat.at[layer], wcat.at[layer], w_sem.at[layer]).wait()

    acts = ((center_in, radius_in), (hidden_center, hidden_radius))
    act_own = [[load(acts[l][x], act.at[l, x, 0], act_sem.at[2 * l + x]) for x in range(2)] for l in range(2)]
    s_one = load(state_one, states.at[0], in_sem.at[3])

    c_grad.wait()
    r_grad.wait()
    s_two.wait()
    for r in (0, rows - 1, *range(1, rows - 1)):
        at = pl.ds(r * width, width)
        sc, sr = relu_back(grads[0, at, :].astype(F32), grads[1, at, :].astype(F32), states[1, at, :])
        skip[0, at, :] = sc
        skip[1, at, :] = sr

    column = lax.broadcasted_iota(jnp.int32, (width, 128), 0)

    def place(layer, x, row, value):
        wide = value.astype(F32)
        later = jnp.where(column == width - 1, 0.0, pltpu.roll(wide, width - 1, 0)).astype(BF16)
        sooner = jnp.where(column == 0, 0.0, pltpu.roll(wide, 1, 0)).astype(BF16)
        for a in range(3):
            r = row - 2 + a
            if 0 <= r < rows:
                for b, shifted in enumerate((later, value, sooner)):
                    cols[layer, x, pl.ds(r * width, width), pl.ds(128 * (3 * a + b), 128)] = shifted

    def place_inside(source, layer):
        for x in range(2):
            for r in range(rows):
                place(layer, x, r + 1, source[x, pl.ds(r * width, width), :])

    def send_halo(source, layer):
        up = pltpu.make_async_remote_copy(
            source.at[:, pl.ds(0, width), :], halo.at[layer, 1],
            halo_ss.at[layer, 0], halo_rs.at[layer, 1], device_id=above, device_id_type=MESH,
        )
        down = pltpu.make_async_remote_copy(
            source.at[:, pl.ds((rows - 1) * width, width), :], halo.at[layer, 0],
            halo_ss.at[layer, 1], halo_rs.at[layer, 0], device_id=below, device_id_type=MESH,
        )
        up.start()
        down.start()
        return up, down

    def place_halo(copies, layer):
        copies[0].wait()
        copies[1].wait()
        top = slab > 0
        bottom = slab < slabs - 1
        for x in range(2):
            above_row = halo[layer, 0, x].astype(F32)
            below_row = halo[layer, 1, x].astype(F32)
            place(layer, x, 0, jnp.where(top, above_row, 0.0).astype(BF16))
            place(layer, x, rows + 1, jnp.where(bottom, below_row, 0.0).astype(BF16))

    def send_act(layer, x):
        copy = pltpu.make_async_remote_copy(
            act.at[layer, x, 0], act.at[layer, x, 1],
            act_ss.at[layer, x], act_rs.at[layer, x], device_id=partner, device_id_type=MESH,
        )
        act_own[layer][x].wait()
        copy.start()
        return copy

    def convolve(layer):
        copies = []
        for x in range(2):
            weight = wcat[layer] if x == 0 else wabs[layer]
            both = lax.dot_general(
                cols[layer, x], weight, (((1,), (1,)), ((), ())), preferred_element_type=F32
            )
            part_own[x] = jnp.where(lower, both[:, :128], both[:, 128:])
            part_send[layer, x] = jnp.where(lower, both[:, 128:], both[:, :128]).astype(BF16)
            copy = pltpu.make_async_remote_copy(
                part_send.at[layer, x], part_recv.at[layer, x],
                part_ss.at[layer, x], part_rs.at[layer, x], device_id=partner, device_id_type=MESH,
            )
            if layer == 1:
                copy.start()
            copies.append(copy)
        return copies

    def turn_own(layer):
        for x in range(2):
            act_t[layer, x, own_at, :] = act[layer, x, 0].T

    def kernel_terms(layer, copies):
        for x in range(2):
            copies[x].wait()
            act_t[layer, x, other_at, :] = act[layer, x, 1].T
        for i in range(3):
            a = jnp.where(first, 2 - i, i)
            at = pl.ds(pl.multiple_of(384 * a, 128), 384)
            kc = jnp.dot(act_t[layer, 0], cols[layer, 0, :, at], preferred_element_type=F32)
            kr = jnp.dot(act_t[layer, 1], cols[layer, 1, :, at], preferred_element_type=F32)
            w = wcat[layer, :, at].astype(F32)
            kr = jnp.where(w > 0.0, kr, jnp.where(w < 0.0, -kr, 0.0))
            k_full[layer, :, at] = scale * (kc + kr)
            if i < 2:
                core_copy(layer, i).start()

    def own_cols(which):
        return pl.ds(pl.multiple_of(which * 512, 512), 640)

    def rows_of(j):
        return pl.ds(pl.multiple_of(j * chunk, chunk), chunk)

    def core_copy(layer, i):
        size = (384, 256)[i]
        src = jnp.where(first, (768, 512)[i], (0, 384)[i])
        dst = jnp.where(first, (256, 0)[i], (0, 384)[i])
        return pltpu.make_async_remote_copy(
            k_full.at[layer, :, pl.ds(pl.multiple_of(src, 128), size)],
            k_recv.at[layer, :, pl.ds(pl.multiple_of(dst, 128), size)],
            core_ss.at[layer, i], core_rs.at[layer, i], device_id=sibling, device_id_type=MESH,
        )

    def one_copy(layer, d):
        j = lax.rem(pos_one + d, members)
        return pltpu.make_async_remote_copy(
            k_mine.at[layer, rows_of(j), :], got_one.at[layer, pos_one],
            one_ss.at[layer, d - 1], one_rs.at[layer, d - 1],
            device_id=one_dev(j), device_id_type=MESH,
        )

    def two_copy(layer, d):
        return pltpu.make_async_remote_copy(
            two.at[layer], got_two.at[layer, pos_two],
            two_ss.at[layer, d - 1], two_rs.at[layer, d - 1],
            device_id=two_dev(lax.rem(pos_two + d, nz)), device_id_type=MESH,
        )

    def back_copy(layer, d):
        j = lax.rem(pos_one + d, members)
        mine = result.at[layer, core, rows_of(pos_one), :]
        return pltpu.make_async_remote_copy(
            mine, mine, back_ss.at[layer, d - 1], back_rs.at[layer, d - 1],
            device_id=one_dev(j), device_id_type=MESH,
        )

    def landed(layer, d):
        j = lax.rem(pos_one - d + members, members)
        return result.at[layer, core, rows_of(j), :]

    def back_from(layer, d):
        there = landed(layer, d)
        return pltpu.make_async_remote_copy(
            there, there, back_ss.at[layer, d - 1], back_rs.at[layer, d - 1],
            device_id=sibling, device_id_type=MESH,
        )

    def fwd_copy(layer, d):
        there = landed(layer, d)
        return pltpu.make_async_remote_copy(
            there, there, fwd_ss.at[layer, d], fwd_rs.at[layer, d],
            device_id=sibling, device_id_type=MESH,
        )

    def fwd_from(layer, d):
        there = result.at[layer, 1 - core, pl.ds(0, chunk), :]
        return pltpu.make_async_remote_copy(
            there, there, fwd_ss.at[layer, d], fwd_rs.at[layer, d],
            device_id=sibling, device_id_type=MESH,
        )

    def scatter(layer):
        for i in range(2):
            core_copy(layer, i).wait()
        own = k_full[layer, :, own_cols(core)]
        k_mine[layer] = (own + k_recv[layer]).astype(BF16)

        @pl.loop(0, members - 1)
        def _(i):
            one_copy(layer, far_first(i, members)).start()

        got_one[layer, pos_one] = k_mine[layer, rows_of(pos_one), :]

    def spread(layer):
        @pl.loop(1, members)
        def _(d):
            one_copy(layer, d).wait()

        total = got_one[layer, 0].astype(F32)
        for j in range(1, members):
            total = total + got_one[layer, j].astype(F32)
        two[layer] = total.astype(BF16)

        @pl.loop(0, nz - 1)
        def _(i):
            two_copy(layer, far_first(i, nz)).start()

        got_two[layer, pos_two] = two[layer]

    def gather(layer):
        @pl.loop(1, nz)
        def _(d):
            two_copy(layer, d).wait()

        total = got_two[layer, 0].astype(F32)
        for j in range(1, nz):
            total = total + got_two[layer, j].astype(F32)
        result[layer, core, rows_of(pos_one), :] = total.astype(BF16)

        @pl.loop(0, members - 1)
        def _(i):
            back_copy(layer, far_first(i, members)).start()

        fwd_copy(layer, 0).start()

    def write_out(layer, which):
        for tap in range(0, 5) if which == 0 else range(5, 9):
            pltpu.make_async_copy(
                result.at[layer, which, :, pl.ds(128 * (tap - 4 * which), 128)],
                out_k.at[layer, tap],
                k_out_sem.at[layer],
            ).start()

    def forward(layer):
        @pl.loop(0, members - 1)
        def _(i):
            d = far_last(i)
            back_from(layer, d).wait_recv()
            fwd_copy(layer, d).start()

    def far_last(i):
        return far_first(members - 2 - i, members)

    def finish(layer):
        @pl.loop(0, members)
        def _(d):
            fwd_from(layer, d).wait_recv()

        write_out(layer, 0)
        write_out(layer, 1)

    def drain(layer):
        @pl.loop(1, members)
        def _(d):
            back_copy(layer, d).wait_send()

        @pl.loop(0, members)
        def _(d):
            fwd_copy(layer, d).wait_send()

    pl.semaphore_wait(barrier, 4 + members - 1 + nz - 1)
    halo_two = send_halo(skip, 1)
    act_one_c = send_act(0, 0)
    load_w(weight_two, 1)
    place_inside(skip, 1)
    load_w(weight_one, 0)
    wait_w(1)
    wabs[1] = jnp.abs(wcat[1])
    place_halo(halo_two, 1)
    part_two = convolve(1)
    act_one = (act_one_c, send_act(0, 1))
    turn_own(0)
    wait_w(0)
    wabs[0] = jnp.abs(wcat[0])
    s_one.wait()

    for copy in part_two:
        copy.wait()
    for r in range(rows):
        at = pl.ds(r * width, width)
        back_c = part_own[0, at, :] + part_recv[1, 0, at, :].astype(F32)
        back_r = part_own[1, at, :] + part_recv[1, 1, at, :].astype(F32)
        ic, ir = relu_back(back_c, back_r, states[0, at, :])
        inner[0, at, :] = ic
        inner[1, at, :] = ir
    halo_one = send_halo(inner, 0)
    act_two = (send_act(1, 0), send_act(1, 1))
    place_inside(inner, 0)
    turn_own(1)
    place_halo(halo_one, 0)

    kernel_terms(0, act_one)
    scatter(0)

    part_one = convolve(0)
    part_one[0].start()

    kernel_terms(1, act_two)
    scatter(1)
    spread(0)
    part_one[1].start()
    spread(1)
    gather(0)
    gather(1)

    outs = []
    for x, out in enumerate((out_c, out_r)):
        part_one[x].wait()
        final[x] = skip[x].astype(F32) + part_own[x] + part_recv[0, x].astype(F32)
        outs.append(load(final.at[x], out, out_sem.at[x]))
    forward(0)
    forward(1)
    finish(0)
    finish(1)
    drain(0)
    drain(1)
    for copy in outs:
        copy.wait()
    for layer in range(2):
        pltpu.make_async_copy(out_k.at[layer], out_k.at[layer], k_out_sem.at[layer]).wait()


def hand_over(made_c, made_r, made_k, out_c, out_r, out_one, out_two, wide, taps, load_sem, sem):
    sources = (made_c, made_r, made_k.at[0], made_k.at[1])
    buffers = (wide.at[0], wide.at[1], taps.at[0], taps.at[1])
    targets = (out_c, out_r, out_one, out_two)
    loads = []
    stores = []
    for i in range(4):
        loads.append(pltpu.make_async_copy(sources[i], buffers[i], load_sem.at[i]))
        stores.append(pltpu.make_async_copy(buffers[i], targets[i], sem.at[i]))
    for copy in loads:
        copy.start()
    for i in range(4):
        loads[i].wait()
        stores[i].start()
    for copy in stores:
        copy.wait()


def body(sizes, *arrays):
    ny, nz, rows, width, _ = sizes
    pix = rows * width
    flat = [a.reshape(pix, 128) for a in arrays[:6]]
    weights = [w.reshape(9, 256, 128) for w in arrays[6:8]]
    grads = [a.reshape(pix, 128) for a in arrays[8:]]
    dma = pltpu.SemaphoreType.DMA
    out_c, out_r, out_k = pl.pallas_call(
        functools.partial(kernel, sizes),
        name="interval_back",
        out_shape=(
            jax.ShapeDtypeStruct((pix, 128), F32),
            jax.ShapeDtypeStruct((pix, 128), F32),
            jax.ShapeDtypeStruct((2, 9, 256, 128), BF16),
        ),
        in_specs=[pl.BlockSpec(memory_space=pl.ANY)] * 10,
        out_specs=(pl.BlockSpec(memory_space=pl.ANY),) * 3,
        scratch_shapes=[
            pltpu.VMEM((2, pix, 128), BF16),
            pltpu.VMEM((2, pix, 128), jnp.int32),
            pltpu.VMEM((2, 256, 1152), BF16),
            pltpu.VMEM((2, 256, 1152), BF16),
            pltpu.VMEM((2, 2, 2, pix, 128), BF16),
            pltpu.VMEM((2, 2, 256, pix), BF16),
            pltpu.VMEM((2, pix, 128), BF16),
            pltpu.VMEM((2, pix, 128), BF16),
            pltpu.VMEM((2, 2, 2, width, 128), BF16),
            pltpu.VMEM((2, 2, pix, 1152), BF16),
            pltpu.VMEM((2, pix, 128), F32),
            pltpu.VMEM((2, 2, pix, 128), BF16),
            pltpu.VMEM((2, 2, pix, 128), BF16),
            pltpu.VMEM((2, pix, 128), F32),
            pltpu.VMEM((2, 256, 1152), F32),
            pltpu.VMEM((2, 256, 640), F32),
            pltpu.VMEM((2, 256, 640), BF16),
            pltpu.VMEM((2, 2 * ny, 128 // ny, 640), BF16),
            pltpu.VMEM((2, 128 // ny, 640), BF16),
            pltpu.VMEM((2, nz, 128 // ny, 640), BF16),
            pltpu.VMEM((2, 2, 256, 640), BF16),
            dma((4,)),
            dma((2,)),
            dma((4,)),
            dma((2, 2)),
            dma((2, 2)),
            dma((2, 2)),
            dma((2, 2)),
            dma((2, 2)),
            dma((2, 2)),
            dma((2, 2)),
            dma((2, 2)),
            dma((2, 2 * ny - 1)),
            dma((2, 2 * ny - 1)),
            dma((2, nz - 1)),
            dma((2, nz - 1)),
            dma((2, 2 * ny - 1)),
            dma((2, 2 * ny - 1)),
            dma((2, 2 * ny)),
            dma((2, 2 * ny)),
            dma((2,)),
            dma((2,)),
        ],
        compiler_params=pltpu.CompilerParams(
            collective_id=0, has_side_effects=True, vmem_limit_bytes=62 << 20
        ),
    )(*flat, *weights, *grads)
    shape = arrays[0].shape
    out_c, out_r, k_one, k_two = pl.pallas_call(
        hand_over,
        name="hand_over",
        out_shape=(
            jax.ShapeDtypeStruct((pix, 128), F32),
            jax.ShapeDtypeStruct((pix, 128), F32),
            jax.ShapeDtypeStruct((9, 256, 128), BF16),
            jax.ShapeDtypeStruct((9, 256, 128), BF16),
        ),
        in_specs=[pl.BlockSpec(memory_space=pl.ANY)] * 3,
        out_specs=(pl.BlockSpec(memory_space=pl.ANY),) * 4,
        scratch_shapes=[
            pltpu.VMEM((2, pix, 128), F32),
            pltpu.VMEM((2, 9, 256, 128), BF16),
            dma((4,)),
            dma((4,)),
        ],
        compiler_params=pltpu.CompilerParams(vmem_limit_bytes=62 << 20),
    )(out_c, out_r, out_k)
    taps = (3, 3, 256, 128)
    return out_c.reshape(shape), out_r.reshape(shape), k_one.reshape(taps), k_two.reshape(taps)


def solution(mesh):
    wide = P("dp", "slab", None, "chan")
    narrow = P(None, None, None, "chan")
    ny, nz = mesh.shape["dp"] // 2, mesh.shape["slab"] // 2

    def whole(*arrays):
        images, height, width, _ = arrays[0].shape
        sizes = (ny, nz, height // (2 * nz), width, 1.0 / math.sqrt(images * height * width))
        return jax.shard_map(
            functools.partial(body, sizes),
            mesh=mesh,
            in_specs=(wide,) * 6 + (narrow,) * 2 + (wide,) * 2,
            out_specs=(wide, wide, narrow, narrow),
            check_vma=False,
        )(*arrays)

    return whole
```

```python
import functools
import math

import jax
import jax.numpy as jnp
from jax import lax
from jax.experimental import pallas as pl
from jax.experimental.pallas import tpu as pltpu
from jax.sharding import PartitionSpec as P

MESH = pl.DeviceIdType.MESH
F32 = jnp.float32
BF16 = jnp.bfloat16


def relu_back(grad_c, grad_r, states):
    average = 0.5 * (grad_c + grad_r)
    keep_c = jnp.where(states == 1, grad_c, jnp.where(states == 2, average, 0.0))
    keep_r = jnp.where(states == 1, grad_r, jnp.where(states == 2, average, 0.0))
    return keep_c.astype(BF16), keep_r.astype(BF16)


def kernel(
    sizes,
    center_in,
    radius_in,
    hidden_center,
    hidden_radius,
    state_one,
    state_two,
    weight_one,
    weight_two,
    grad_center,
    grad_radius,
    out_c,
    out_r,
    out_k,
    grads,
    states,
    wcat,
    wabs,
    act,
    act_t,
    skip,
    inner,
    halo,
    cols,
    part_own,
    part_send,
    part_recv,
    final,
    k_full,
    k_recv,
    k_mine,
    got_one,
    two,
    got_two,
    result,
    in_sem,
    w_sem,
    act_sem,
    halo_ss,
    halo_rs,
    act_ss,
    act_rs,
    part_ss,
    part_rs,
    core_ss,
    core_rs,
    one_ss,
    one_rs,
    two_ss,
    two_rs,
    back_ss,
    back_rs,
    fwd_ss,
    fwd_rs,
    out_sem,
    k_out_sem,
):
    ny, nz, rows, width, scale = sizes
    pix = rows * width
    dp, slab, chan = lax.axis_index("dp"), lax.axis_index("slab"), lax.axis_index("chan")
    y, core = lax.div(dp, 2), lax.rem(dp, 2)
    z, x_lo = lax.div(slab, 2), lax.rem(slab, 2)
    slabs = 2 * nz
    first = core == 0
    members = 2 * ny
    chunk = 256 // members
    pos_one = jnp.where(first, y, z) * 2 + x_lo
    pos_two = jnp.where(first, z, y)

    def one_dev(j):
        a, x = lax.div(j, 2), lax.rem(j, 2)
        return (jnp.where(first, a, y) * 2 + core, jnp.where(first, z, a) * 2 + x, chan)

    def two_dev(j):
        return (jnp.where(first, y, j) * 2 + core, jnp.where(first, j, z) * 2 + x_lo, chan)

    partner = (dp, slab, 1 - chan)
    sibling = (y * 2 + 1 - core, slab, chan)
    above = (dp, lax.rem(slab + slabs - 1, slabs), chan)
    below = (dp, lax.rem(slab + 1, slabs), chan)

    def load(src, dst, sem):
        copy = pltpu.make_async_copy(src, dst, sem)
        copy.start()
        return copy

    c_grad = load(grad_center, grads.at[0], in_sem.at[0])
    r_grad = load(grad_radius, grads.at[1], in_sem.at[1])
    s_two = load(state_two, states.at[1], in_sem.at[2])

    def far_first(i, count):
        k = lax.div(i + 1, 2)
        return count // 2 + jnp.where(lax.rem(i, 2) == 1, k, -k)

    barrier = pltpu.get_barrier_semaphore()

    @pl.loop(0, members - 1)
    def _(i):
        d = far_first(i, members)
        peer = one_dev(lax.rem(pos_one + d, members))
        pl.semaphore_signal(barrier, inc=1, device_id=peer, device_id_type=MESH)

    @pl.loop(0, nz - 1)
    def _(i):
        peer = two_dev(lax.rem(pos_two + far_first(i, nz), nz))
        pl.semaphore_signal(barrier, inc=1, device_id=peer, device_id_type=MESH)

    for peer in (partner, above, below, sibling):
        pl.semaphore_signal(barrier, inc=1, device_id=peer, device_id_type=MESH)

    own_at = pl.ds(pl.multiple_of(chan * 128, 128), 128)
    other_at = pl.ds(pl.multiple_of((1 - chan) * 128, 128), 128)
    lower = chan == 0

    def load_w(src, layer):
        for tap in range(9):
            pltpu.make_async_copy(
                src.at[tap], wcat.at[layer, :, pl.ds(128 * tap, 128)], w_sem.at[layer]
            ).start()

    def wait_w(layer):
        pltpu.make_async_copy(wcat.at[layer], wcat.at[layer], w_sem.at[layer]).wait()

    acts = ((center_in, radius_in), (hidden_center, hidden_radius))
    act_own = [[load(acts[l][x], act.at[l, x, 0], act_sem.at[2 * l + x]) for x in range(2)] for l in range(2)]
    s_one = load(state_one, states.at[0], in_sem.at[3])

    c_grad.wait()
    r_grad.wait()
    s_two.wait()
    for r in (0, rows - 1, *range(1, rows - 1)):
        at = pl.ds(r * width, width)
        sc, sr = relu_back(grads[0, at, :].astype(F32), grads[1, at, :].astype(F32), states[1, at, :])
        skip[0, at, :] = sc
        skip[1, at, :] = sr

    column = lax.broadcasted_iota(jnp.int32, (width, 128), 0)

    def place(layer, x, row, value):
        wide = value.astype(F32)
        later = jnp.where(column == width - 1, 0.0, pltpu.roll(wide, width - 1, 0)).astype(BF16)
        sooner = jnp.where(column == 0, 0.0, pltpu.roll(wide, 1, 0)).astype(BF16)
        for a in range(3):
            r = row - 2 + a
            if 0 <= r < rows:
                for b, shifted in enumerate((later, value, sooner)):
                    cols[layer, x, pl.ds(r * width, width), pl.ds(128 * (3 * a + b), 128)] = shifted

    def place_inside(source, layer):
        for x in range(2):
            for r in range(rows):
                place(layer, x, r + 1, source[x, pl.ds(r * width, width), :])

    def send_halo(source, layer):
        up = pltpu.make_async_remote_copy(
            source.at[:, pl.ds(0, width), :], halo.at[layer, 1],
            halo_ss.at[layer, 0], halo_rs.at[layer, 1], device_id=above, device_id_type=MESH,
        )
        down = pltpu.make_async_remote_copy(
            source.at[:, pl.ds((rows - 1) * width, width), :], halo.at[layer, 0],
            halo_ss.at[layer, 1], halo_rs.at[layer, 0], device_id=below, device_id_type=MESH,
        )
        up.start()
        down.start()
        return up, down

    def place_halo(copies, layer):
        copies[0].wait()
        copies[1].wait()
        top = slab > 0
        bottom = slab < slabs - 1
        for x in range(2):
            above_row = halo[layer, 0, x].astype(F32)
            below_row = halo[layer, 1, x].astype(F32)
            place(layer, x, 0, jnp.where(top, above_row, 0.0).astype(BF16))
            place(layer, x, rows + 1, jnp.where(bottom, below_row, 0.0).astype(BF16))

    def send_act(layer, x):
        copy = pltpu.make_async_remote_copy(
            act.at[layer, x, 0], act.at[layer, x, 1],
            act_ss.at[layer, x], act_rs.at[layer, x], device_id=partner, device_id_type=MESH,
        )
        act_own[layer][x].wait()
        copy.start()
        return copy

    def convolve(layer):
        copies = []
        for x in range(2):
            weight = wcat[layer] if x == 0 else wabs[layer]
            both = lax.dot_general(
                cols[layer, x], weight, (((1,), (1,)), ((), ())), preferred_element_type=F32
            )
            part_own[x] = jnp.where(lower, both[:, :128], both[:, 128:])
            part_send[layer, x] = jnp.where(lower, both[:, 128:], both[:, :128]).astype(BF16)
            copy = pltpu.make_async_remote_copy(
                part_send.at[layer, x], part_recv.at[layer, x],
                part_ss.at[layer, x], part_rs.at[layer, x], device_id=partner, device_id_type=MESH,
            )
            if layer == 1:
                copy.start()
            copies.append(copy)
        return copies

    def turn_own(layer):
        for x in range(2):
            act_t[layer, x, own_at, :] = act[layer, x, 0].T

    def kernel_terms(layer, copies):
        for x in range(2):
            copies[x].wait()
            act_t[layer, x, other_at, :] = act[layer, x, 1].T
        for i in range(3):
            a = jnp.where(first, 2 - i, i)
            at = pl.ds(pl.multiple_of(384 * a, 128), 384)
            kc = jnp.dot(act_t[layer, 0], cols[layer, 0, :, at], preferred_element_type=F32)
            kr = jnp.dot(act_t[layer, 1], cols[layer, 1, :, at], preferred_element_type=F32)
            w = wcat[layer, :, at].astype(F32)
            kr = jnp.where(w > 0.0, kr, jnp.where(w < 0.0, -kr, 0.0))
            k_full[layer, :, at] = scale * (kc + kr)
            if i < 2:
                core_copy(layer, i).start()

    def own_cols(which):
        return pl.ds(pl.multiple_of(which * 512, 512), 640)

    def rows_of(j):
        return pl.ds(pl.multiple_of(j * chunk, chunk), chunk)

    def core_copy(layer, i):
        size = (384, 256)[i]
        src = jnp.where(first, (768, 512)[i], (0, 384)[i])
        dst = jnp.where(first, (256, 0)[i], (0, 384)[i])
        return pltpu.make_async_remote_copy(
            k_full.at[layer, :, pl.ds(pl.multiple_of(src, 128), size)],
            k_recv.at[layer, :, pl.ds(pl.multiple_of(dst, 128), size)],
            core_ss.at[layer, i], core_rs.at[layer, i], device_id=sibling, device_id_type=MESH,
        )

    def one_copy(layer, d):
        j = lax.rem(pos_one + d, members)
        return pltpu.make_async_remote_copy(
            k_mine.at[layer, rows_of(j), :], got_one.at[layer, pos_one],
            one_ss.at[layer, d - 1], one_rs.at[layer, d - 1],
            device_id=one_dev(j), device_id_type=MESH,
        )

    def two_copy(layer, d):
        return pltpu.make_async_remote_copy(
            two.at[layer], got_two.at[layer, pos_two],
            two_ss.at[layer, d - 1], two_rs.at[layer, d - 1],
            device_id=two_dev(lax.rem(pos_two + d, nz)), device_id_type=MESH,
        )

    def back_copy(layer, d):
        j = lax.rem(pos_one + d, members)
        mine = result.at[layer, core, rows_of(pos_one), :]
        return pltpu.make_async_remote_copy(
            mine, mine, back_ss.at[layer, d - 1], back_rs.at[layer, d - 1],
            device_id=one_dev(j), device_id_type=MESH,
        )

    def landed(layer, d):
        j = lax.rem(pos_one - d + members, members)
        return result.at[layer, core, rows_of(j), :]

    def back_from(layer, d):
        there = landed(layer, d)
        return pltpu.make_async_remote_copy(
            there, there, back_ss.at[layer, d - 1], back_rs.at[layer, d - 1],
            device_id=sibling, device_id_type=MESH,
        )

    def fwd_copy(layer, d):
        there = landed(layer, d)
        return pltpu.make_async_remote_copy(
            there, there, fwd_ss.at[layer, d], fwd_rs.at[layer, d],
            device_id=sibling, device_id_type=MESH,
        )

    def fwd_from(layer, d):
        there = result.at[layer, 1 - core, pl.ds(0, chunk), :]
        return pltpu.make_async_remote_copy(
            there, there, fwd_ss.at[layer, d], fwd_rs.at[layer, d],
            device_id=sibling, device_id_type=MESH,
        )

    def scatter(layer):
        for i in range(2):
            core_copy(layer, i).wait()
        own = k_full[layer, :, own_cols(core)]
        k_mine[layer] = (own + k_recv[layer]).astype(BF16)

        @pl.loop(0, members - 1)
        def _(i):
            one_copy(layer, far_first(i, members)).start()

        got_one[layer, pos_one] = k_mine[layer, rows_of(pos_one), :]

    def spread(layer):
        @pl.loop(1, members)
        def _(d):
            one_copy(layer, d).wait()

        total = got_one[layer, 0].astype(F32)
        for j in range(1, members):
            total = total + got_one[layer, j].astype(F32)
        two[layer] = total.astype(BF16)

        @pl.loop(0, nz - 1)
        def _(i):
            two_copy(layer, far_first(i, nz)).start()

        got_two[layer, pos_two] = two[layer]

    def gather(layer):
        @pl.loop(1, nz)
        def _(d):
            two_copy(layer, d).wait()

        total = got_two[layer, 0].astype(F32)
        for j in range(1, nz):
            total = total + got_two[layer, j].astype(F32)
        result[layer, core, rows_of(pos_one), :] = total.astype(BF16)

        @pl.loop(0, members - 1)
        def _(i):
            back_copy(layer, far_first(i, members)).start()

        fwd_copy(layer, 0).start()

    def write_out(layer, which):
        for tap in range(0, 5) if which == 0 else range(5, 9):
            pltpu.make_async_copy(
                result.at[layer, which, :, pl.ds(128 * (tap - 4 * which), 128)],
                out_k.at[layer, tap],
                k_out_sem.at[layer],
            ).start()

    def deliver(layer):
        @pl.loop(1, members)
        def _(d):
            back_from(layer, d).wait_recv()
            fwd_copy(layer, d).start()

        @pl.when(first)
        def _():
            write_out(layer, 0)

        @pl.when(core == 1)
        def _():
            write_out(layer, 1)

        @pl.loop(0, members)
        def _(d):
            fwd_from(layer, d).wait_recv()

        @pl.when(first)
        def _():
            write_out(layer, 1)

        @pl.when(core == 1)
        def _():
            write_out(layer, 0)

        @pl.loop(1, members)
        def _(d):
            back_copy(layer, d).wait_send()

        @pl.loop(0, members)
        def _(d):
            fwd_copy(layer, d).wait_send()

    pl.semaphore_wait(barrier, 4 + members - 1 + nz - 1)
    halo_two = send_halo(skip, 1)
    act_one_c = send_act(0, 0)
    load_w(weight_two, 1)
    place_inside(skip, 1)
    load_w(weight_one, 0)
    wait_w(1)
    wabs[1] = jnp.abs(wcat[1])
    place_halo(halo_two, 1)
    part_two = convolve(1)
    act_one = (act_one_c, send_act(0, 1))
    turn_own(0)
    wait_w(0)
    wabs[0] = jnp.abs(wcat[0])
    s_one.wait()

    for copy in part_two:
        copy.wait()
    for r in range(rows):
        at = pl.ds(r * width, width)
        back_c = part_own[0, at, :] + part_recv[1, 0, at, :].astype(F32)
        back_r = part_own[1, at, :] + part_recv[1, 1, at, :].astype(F32)
        ic, ir = relu_back(back_c, back_r, states[0, at, :])
        inner[0, at, :] = ic
        inner[1, at, :] = ir
    halo_one = send_halo(inner, 0)
    act_two = (send_act(1, 0), send_act(1, 1))
    place_inside(inner, 0)
    turn_own(1)
    place_halo(halo_one, 0)

    kernel_terms(0, act_one)
    scatter(0)

    kernel_terms(1, act_two)
    scatter(1)
    part_one = convolve(0)
    spread(0)
    for copy in part_one:
        copy.start()
    spread(1)
    gather(0)
    gather(1)

    outs = []
    for x, out in enumerate((out_c, out_r)):
        part_one[x].wait()
        final[x] = skip[x].astype(F32) + part_own[x] + part_recv[0, x].astype(F32)
        outs.append(load(final.at[x], out, out_sem.at[x]))
    deliver(0)
    deliver(1)
    for copy in outs:
        copy.wait()
    for layer in range(2):
        pltpu.make_async_copy(out_k.at[layer], out_k.at[layer], k_out_sem.at[layer]).wait()


def hand_over(made_c, made_r, made_k, out_c, out_r, out_one, out_two, wide, taps, load_sem, sem):
    half = wide.shape[1] // 2
    loads = []
    stores = []

    def add(source, buffer, target):
        i = len(loads)
        loads.append(pltpu.make_async_copy(source, buffer, load_sem.at[i]))
        stores.append(pltpu.make_async_copy(buffer, target, sem.at[i]))
        loads[i].start()

    for layer, target in enumerate((out_one, out_two)):
        for part in range(3):
            at = pl.ds(3 * part, 3)
            add(made_k.at[layer, at], taps.at[layer, at], target.at[at])
    for i, (source, target) in enumerate(((made_c, out_c), (made_r, out_r))):
        for part in range(2):
            at = pl.ds(half * part, half)
            add(source.at[at], wide.at[i, at], target.at[at])
    for load, store in zip(loads, stores):
        load.wait()
        store.start()
    for store in stores:
        store.wait()


def body(sizes, *arrays):
    ny, nz, rows, width, _ = sizes
    pix = rows * width
    flat = [a.reshape(pix, 128) for a in arrays[:6]]
    weights = [w.reshape(9, 256, 128) for w in arrays[6:8]]
    grads = [a.reshape(pix, 128) for a in arrays[8:]]
    dma = pltpu.SemaphoreType.DMA
    out_c, out_r, out_k = pl.pallas_call(
        functools.partial(kernel, sizes),
        name="interval_back",
        out_shape=(
            jax.ShapeDtypeStruct((pix, 128), F32),
            jax.ShapeDtypeStruct((pix, 128), F32),
            jax.ShapeDtypeStruct((2, 9, 256, 128), BF16),
        ),
        in_specs=[pl.BlockSpec(memory_space=pl.ANY)] * 10,
        out_specs=(pl.BlockSpec(memory_space=pl.ANY),) * 3,
        scratch_shapes=[
            pltpu.VMEM((2, pix, 128), BF16),
            pltpu.VMEM((2, pix, 128), jnp.int32),
            pltpu.VMEM((2, 256, 1152), BF16),
            pltpu.VMEM((2, 256, 1152), BF16),
            pltpu.VMEM((2, 2, 2, pix, 128), BF16),
            pltpu.VMEM((2, 2, 256, pix), BF16),
            pltpu.VMEM((2, pix, 128), BF16),
            pltpu.VMEM((2, pix, 128), BF16),
            pltpu.VMEM((2, 2, 2, width, 128), BF16),
            pltpu.VMEM((2, 2, pix, 1152), BF16),
            pltpu.VMEM((2, pix, 128), F32),
            pltpu.VMEM((2, 2, pix, 128), BF16),
            pltpu.VMEM((2, 2, pix, 128), BF16),
            pltpu.VMEM((2, pix, 128), F32),
            pltpu.VMEM((2, 256, 1152), F32),
            pltpu.VMEM((2, 256, 640), F32),
            pltpu.VMEM((2, 256, 640), BF16),
            pltpu.VMEM((2, 2 * ny, 128 // ny, 640), BF16),
            pltpu.VMEM((2, 128 // ny, 640), BF16),
            pltpu.VMEM((2, nz, 128 // ny, 640), BF16),
            pltpu.VMEM((2, 2, 256, 640), BF16),
            dma((4,)),
            dma((2,)),
            dma((4,)),
            dma((2, 2)),
            dma((2, 2)),
            dma((2, 2)),
            dma((2, 2)),
            dma((2, 2)),
            dma((2, 2)),
            dma((2, 2)),
            dma((2, 2)),
            dma((2, 2 * ny - 1)),
            dma((2, 2 * ny - 1)),
            dma((2, nz - 1)),
            dma((2, nz - 1)),
            dma((2, 2 * ny - 1)),
            dma((2, 2 * ny - 1)),
            dma((2, 2 * ny)),
            dma((2, 2 * ny)),
            dma((2,)),
            dma((2,)),
        ],
        compiler_params=pltpu.CompilerParams(
            collective_id=0, has_side_effects=True, vmem_limit_bytes=62 << 20
        ),
    )(*flat, *weights, *grads)
    shape = arrays[0].shape
    out_c, out_r, k_one, k_two = pl.pallas_call(
        hand_over,
        name="hand_over",
        out_shape=(
            jax.ShapeDtypeStruct((pix, 128), F32),
            jax.ShapeDtypeStruct((pix, 128), F32),
            jax.ShapeDtypeStruct((9, 256, 128), BF16),
            jax.ShapeDtypeStruct((9, 256, 128), BF16),
        ),
        in_specs=[pl.BlockSpec(memory_space=pl.ANY)] * 3,
        out_specs=(pl.BlockSpec(memory_space=pl.ANY),) * 4,
        scratch_shapes=[
            pltpu.VMEM((2, pix, 128), F32),
            pltpu.VMEM((2, 9, 256, 128), BF16),
            dma((10,)),
            dma((10,)),
        ],
        compiler_params=pltpu.CompilerParams(vmem_limit_bytes=62 << 20),
    )(out_c, out_r, out_k)
    taps = (3, 3, 256, 128)
    return out_c.reshape(shape), out_r.reshape(shape), k_one.reshape(taps), k_two.reshape(taps)


def solution(mesh):
    wide = P("dp", "slab", None, "chan")
    narrow = P(None, None, None, "chan")
    ny, nz = mesh.shape["dp"] // 2, mesh.shape["slab"] // 2

    def whole(*arrays):
        images, height, width, _ = arrays[0].shape
        sizes = (ny, nz, height // (2 * nz), width, 1.0 / math.sqrt(images * height * width))
        return jax.shard_map(
            functools.partial(body, sizes),
            mesh=mesh,
            in_specs=(wide,) * 6 + (narrow,) * 2 + (wide,) * 2,
            out_specs=(wide, wide, narrow, narrow),
            check_vma=False,
        )(*arrays)

    return whole
```
